256 devices in a mesh: slab: 32 (over x, z), rows: 8 (over y, core).
Axes of the slice: x: 4, y: 4, z: 8, core: 2. Of those that a mesh axis runs over, the one named last changes fastest.
Arguments:
- blocks: float32 [1536, 64, 4096], P(('slab', 'rows')), may hold values from -6 to 6
- coords: int32 [1536, 3], P(('slab', 'rows')), may hold values from 0 to 255, as said below
- counts: int32 [256], P(('slab', 'rows')), may hold values from 0 to 6, as said below
- factor_b: float32 [16384, 64], P('rows'), may hold values from -0.055242717 to 0.055242717
- factor_c: float32 [16384, 64], P(('slab', 'rows')), may hold values from -0.055242717 to 0.055242717
Outputs:
- factor_a_new: float32 [16384, 64], P('rows')
- factor_b_new: float32 [16384, 64], P('rows')
- scale_b: float32 [64], replicated
The draws below stay inside these ranges and needn't reach their ends.
Inputs may be any that keep to these rules, and one draw needn't show every extreme that they name: Slot k of device d holds part of the tensor when k < counts[d]; the other slots hold data that is not part of it. In every draw some device has all 6 slots live. `coords`: every slot of the device with index g along rows (in the joined slab+rows order, slab slowest) has its first two coordinates in the range from g * 16384 // (64 * the number of devices along rows) up to the next such bound; the third coordinate is free.
All inputs are finite; a program needn't handle non-finite values.
Results may differ from the reference program's by a relative error of at most 0.00025.
Values sent between devices are 32-bit elements; how exact they have to be, the bound alone decides.
No kernel may reach another device: no remote copies, remote signals or barrier semaphores. Data moves between devices by JAX's collectives and lax.ppermute only.
A program may use at most 64 MiB of HBM per device.

```python
import jax
import jax.numpy as jnp
from jax import lax

I = 16384
R = 64
BS = 64
CAP = 6
NDEV = 256
SLOTS = 1536
N_ROWS = 8


def factor_law(key, low, high):
    part_one, part_two, part_three = jax.random.split(key, 3)
    common = jnp.clip(jax.random.normal(part_one, (I, 1), jnp.float32), -4.0, 4.0)
    noise = jnp.clip(jax.random.normal(part_two, (I, R), jnp.float32), -4.0, 4.0)
    row_scale = jnp.exp(jax.random.uniform(part_three, (I, 1), jnp.float32, jnp.log(low), jnp.log(high)))
    raw = row_scale * (common + noise)
    return (jnp.clip(raw, -10.0, 10.0) / jnp.sqrt(2.0 * I)).astype(jnp.float32)


def draw_factor_b(key, part):
    key = jax.random.fold_in(key, 11)
    return factor_law(key, 0.3, 3.0)


def draw_factor_c(key, part):
    key = jax.random.fold_in(key, 23)
    return factor_law(key, 0.3, 3.0)


def draw_counts(key, part):
    key = jax.random.fold_in(key, 37)
    first_key, second_key, third_key = jax.random.split(key, 3)
    picker = jax.random.randint(first_key, (NDEV,), 0, 10)
    lighter = jax.random.randint(second_key, (NDEV,), 0, CAP // 2 + 1)
    loads = jnp.where(picker < 3, CAP, lighter).astype(jnp.int32)
    fullest = jax.random.randint(third_key, (), 0, NDEV)
    return loads.at[fullest].set(CAP).astype(jnp.int32)


def draw_coords(key, part):
    key = jax.random.fold_in(key, 51)
    key_one, key_two, key_three, key_four, key_five = jax.random.split(key, 5)
    slot_ids = jnp.arange(SLOTS, dtype=jnp.int32)
    group = slot_ids // CAP % N_ROWS
    per_group = I // (BS * N_ROWS)
    first = group * per_group + jax.random.randint(key_one, (SLOTS,), 0, per_group)
    second = group * per_group + jax.random.randint(key_two, (SLOTS,), 0, per_group)
    third = jax.random.randint(key_three, (SLOTS,), 0, I // BS)
    top_slot = jax.random.randint(key_four, (), 0, SLOTS)
    low_slot = (top_slot + 1 + jax.random.randint(key_five, (), 0, SLOTS - 1)) % SLOTS
    third = third.at[top_slot].set(I // BS - 1)
    third = third.at[low_slot].set(0)
    return jnp.stack([first, second, third], axis=1).astype(jnp.int32)


def levels(key, extent, cuts, smallest, largest):
    def one(axis_at, parts):
        heights = jax.random.uniform(jax.random.fold_in(jax.random.fold_in(key, 6), axis_at), (parts,), jnp.float32, smallest / len(cuts), largest / len(cuts))
        return jnp.repeat(jnp.exp(heights), extent[axis_at] // parts).reshape((-1,) + (1,) * (len(extent) - axis_at - 1))

    loudness = one(*cuts[0])
    for cut in cuts[1:]:
        loudness = loudness * one(*cut)
    return loudness


def bell_draw(rng, shape, width, bound, pieces=(), held_as=jnp.bfloat16):
    result = jax.random.normal(rng, shape, jnp.float32) * width
    if len(pieces) > 0:
        result = levels(rng, shape, pieces, -0.22, 0.18) * result
    return jnp.clip(result, min=-bound, max=bound).astype(held_as)


def setup_inputs(seed: int = 0) -> dict:
    streams_of = jax.random.split(jax.random.key(seed), 6)
    blocks = bell_draw(streams_of[0], (SLOTS, BS, BS * BS), 1.0, 6.0, ((0, 256),), jnp.float32)
    coords = draw_coords(jax.random.fold_in(streams_of[5], 71), 0)
    counts = draw_counts(jax.random.fold_in(streams_of[5], 71), 0)
    factor_b = draw_factor_b(jax.random.fold_in(streams_of[5], 71), 0)
    factor_c = draw_factor_c(jax.random.fold_in(streams_of[5], 71), 0)
    return dict(blocks=blocks, coords=coords, counts=counts, factor_b=factor_b, factor_c=factor_c)


def apply_inverse(rows, gram):
    chol = jnp.linalg.cholesky(gram)
    inner = lax.linalg.triangular_solve(chol, rows, left_side=False, lower=True, transpose_a=True)
    return lax.linalg.triangular_solve(chol, inner, left_side=False, lower=True, transpose_a=False)

def contract(blocks, coords, live, first, third, mode):

    def step(acc, item):
        block, place, flag = item
        third_rows = lax.dynamic_slice_in_dim(third, place[2] * BS, BS, 0)
        folded = jnp.dot(block.reshape(BS * BS, BS).astype(jnp.float32), third_rows.astype(jnp.float32), precision=lax.Precision.HIGHEST, preferred_element_type=jnp.float32).reshape(BS, BS, R)
        if mode == 1:
            second = lax.dynamic_slice_in_dim(first, place[1] * BS, BS, 0)
            term = jnp.einsum('ijr,jr->ir', folded, second, precision=lax.Precision.HIGHEST)
            target = place[0] * BS
        else:
            second = lax.dynamic_slice_in_dim(first, place[0] * BS, BS, 0)
            term = jnp.einsum('ijr,ir->jr', folded, second, precision=lax.Precision.HIGHEST)
            target = place[1] * BS
        current = lax.dynamic_slice_in_dim(acc, target, BS, 0)
        acc = lax.dynamic_update_slice_in_dim(acc, current + flag * term, target, 0)
        return (acc, None)
    start = jnp.zeros((I, R), jnp.float32)
    total, _ = lax.scan(step, start, (blocks, coords, live))
    return total

def update(mttkrp, gram):
    solved = apply_inverse(mttkrp, gram)
    scale = jnp.sqrt(lax.optimization_barrier(jnp.sum(solved * solved, axis=0)) / I + 1e-06)
    return (solved / scale, scale)

def reference(blocks, coords, counts, factor_b, factor_c):
    slot_ids = jnp.arange(SLOTS, dtype=jnp.int32)
    owner = slot_ids // CAP
    live = (slot_ids % CAP < counts[owner]).astype(jnp.float32)
    high = lax.Precision.HIGHEST
    gram_b = jnp.dot(factor_b.T.astype(jnp.float32), factor_b.astype(jnp.float32), precision=high, preferred_element_type=jnp.float32)
    gram_c = jnp.dot(factor_c.T.astype(jnp.float32), factor_c.astype(jnp.float32), precision=high, preferred_element_type=jnp.float32)
    mttkrp_a = contract(blocks, coords, live, factor_b, factor_c, 1)
    factor_a_new, scale_a = update(mttkrp_a, gram_b * gram_c)
    gram_a = jnp.dot(factor_a_new.T.astype(jnp.float32), factor_a_new.astype(jnp.float32), precision=high, preferred_element_type=jnp.float32)
    mttkrp_b = contract(blocks, coords, live, factor_a_new, factor_c, 2)
    factor_b_new, scale_b = update(mttkrp_b, gram_a * gram_c)
    return (factor_a_new, factor_b_new, scale_b)
```

```python
import jax
import jax.numpy as jnp
from jax import lax
from jax.experimental import pallas as pl
from jax.experimental.pallas import tpu as pltpu
from jax.sharding import PartitionSpec as P

SIDE = 64
HALF = 32
WIDE = 128
SLOTS = 6
PEERS = 8
OWNERS = 32
GROUP = 2048
ROWS = 16384
HIGH = lax.Precision.HIGHEST
LIMIT = pltpu.CompilerParams(vmem_limit_bytes=48 * 1024 * 1024)


def low(shape):
    return lax.broadcasted_iota(jnp.int32, shape, 1) < SIDE


def swap(x):
    return pltpu.roll(x, SIDE, 1)


def unfold_halves(packed):
    mask, other = low(packed.shape), swap(packed)
    return jnp.concatenate([jnp.where(mask, packed, other), jnp.where(mask, other, packed)], axis=0)


def fold_halves(rows):
    return jnp.where(low((HALF, WIDE)), rows[:HALF], rows[HALF:])


def gram_packed(packed):
    both = lax.dot_general(
        packed, packed, (((0,), (0,)), ((), ())), precision=HIGH, preferred_element_type=jnp.float32
    )
    total = both[:SIDE] + swap(both[SIDE:])
    return jnp.where(low(total.shape), total, swap(total))


def inverse(gram):
    shape = gram.shape
    row = lax.broadcasted_iota(jnp.int32, shape, 0)
    lane = lax.broadcasted_iota(jnp.int32, shape, 1)
    work = jnp.where(lane < SIDE, gram, jnp.where(lane - SIDE == row, 1.0, 0.0))
    for k in range(SIDE):
        line = work[k : k + 1, :] / work[k : k + 1, k : k + 1]
        column = work[:, k : k + 1]
        work = jnp.where(row == k, line, work - column * line)
    return work


def prepare(second_ref, third_ref, spread_ref, gram_ref):
    second = second_ref[...]
    twice = jnp.concatenate([second, second], axis=0)
    gram_ref[...] = lax.dot_general(
        second, twice, (((1,), (1,)), ((), ())), precision=HIGH, preferred_element_type=jnp.float32
    )
    third = third_ref[...]
    packed = jnp.concatenate([third[:HALF], third[HALF:]], axis=1)
    spread_ref[...] = jnp.broadcast_to(packed[None], spread_ref.shape)


def answer(asked_ref, third_ref, gram_ref, out_ref):
    for peer in range(PEERS):
        for slot in range(SLOTS):
            block = asked_ref[peer, slot] // PEERS
            out_ref[peer, slot * HALF : (slot + 1) * HALF, :] = third_ref[block]
    third = third_ref[...].reshape(OWNERS * HALF, WIDE)
    grams = jnp.where(low((SIDE, WIDE)), gram_ref[...], gram_packed(third))
    out_ref[:, SLOTS * HALF :, :] = jnp.broadcast_to(grams[None], (PEERS, SIDE, WIDE))


def split(x):
    high = x.astype(jnp.bfloat16)
    return high, (x - high.astype(jnp.float32)).astype(jnp.bfloat16)


def fold(
    place_ref, count_ref, block_ref, third_ref, second_ref, folded_ref, part_ref, inverse_ref, gram_ref, turned
):
    slot = pl.program_id(0)

    @pl.when(slot == 0)
    def _():
        part_ref[...] = jnp.zeros_like(part_ref)
        grams = jnp.sum(third_ref[:, SLOTS * HALF :, :], axis=0)
        mask = low(grams.shape)
        other = swap(grams)
        gram_ref[...] = jnp.where(mask, other, grams)
        solved = inverse(grams * other)
        inverse_ref[:SIDE, :] = jnp.where(mask, swap(solved), 0.0)
        inverse_ref[SIDE:, :] = jnp.where(mask, 0.0, solved)

    @pl.when(slot < count_ref[0])
    def _():
        which = place_ref[slot, 2]
        packed = third_ref[which % PEERS, pl.ds(slot * HALF, HALF), :]
        mask, other = low(packed.shape), swap(packed)
        zero = jnp.zeros_like(packed)
        twin = jnp.concatenate(
            [
                jnp.where(mask, packed, zero),
                jnp.where(mask, other, zero),
                jnp.where(mask, zero, other),
                jnp.where(mask, zero, packed),
            ],
            axis=0,
        )
        high, rest = split(twin)
        weights = jnp.concatenate([high, rest], axis=1)
        weights = jnp.concatenate([weights, weights], axis=0)
        place = place_ref[slot, 1] % OWNERS
        tile = second_ref[:, pl.ds(pl.multiple_of(place // 2 * WIDE, WIDE), WIDE)]
        turned[...] = jnp.concatenate([tile, tile], axis=0).T
        start = place % 2 * SIDE
        pairs = jnp.where(
            mask, turned[pl.ds(start, HALF, stride=2), :], turned[pl.ds(start + 1, HALF, stride=2), :]
        )
        total = jnp.zeros((SIDE, WIDE), jnp.float32)
        step = 8
        for at in range(0, HALF, step):
            lines = jnp.concatenate(
                [block_ref[0, :, (at + n) * WIDE : (at + n + 1) * WIDE] for n in range(step)], axis=0
            )
            high, rest = split(lines)
            lines = jnp.concatenate([high, rest], axis=1)
            product = jnp.dot(lines, weights, preferred_element_type=jnp.float32)
            product = product[:, :WIDE] + product[:, WIDE:]
            for n in range(step):
                piece = product[n * SIDE : (n + 1) * SIDE]
                folded_ref[0, at + n] = piece
                total += piece * pairs[at + n : at + n + 1, :]
        total = total + swap(total)
        part_ref[place_ref[slot, 0] % OWNERS] += fold_halves(total)


def solve_first(part_ref, inverse_ref, out_ref):
    total = jnp.sum(part_ref[...], axis=0)
    solved = jnp.dot(total, inverse_ref[...], precision=HIGH, preferred_element_type=jnp.float32)
    out_ref[...] = jnp.broadcast_to(solved[None], out_ref.shape)


def contract(place_ref, count_ref, folded_ref, first_ref, part_ref, square_ref):
    slot = pl.program_id(0)

    @pl.when(slot == 0)
    def _():
        part_ref[...] = jnp.zeros_like(part_ref)
        square = fold_halves(gram_packed(first_ref[...].reshape(OWNERS * HALF, WIDE)))
        square_ref[...] = jnp.broadcast_to(square[None], square_ref.shape)

    @pl.when(slot < count_ref[0])
    def _():
        first = unfold_halves(first_ref[place_ref[slot, 0] % OWNERS])
        term = jnp.sum(folded_ref[0] * first[None], axis=1)
        part_ref[place_ref[slot, 1] % OWNERS] += term


def solve_second(part_ref, square_ref, gram_ref, first_ref, out_ref, new_ref, spread):
    square = unfold_halves(jnp.sum(square_ref[...], axis=0))
    shape = square.shape
    row = lax.broadcasted_iota(jnp.int32, shape, 0)
    lane = lax.broadcasted_iota(jnp.int32, shape, 1)
    means = jnp.where(row == lane % SIDE, square, 0.0) / ROWS
    along = jnp.sqrt(jnp.sum(means, axis=0, keepdims=True) + 1e-06)
    down = jnp.sqrt(jnp.sum(jnp.where(lane < SIDE, means, 0.0), axis=1, keepdims=True) + 1e-06)
    gram = square / along / down * gram_ref[...]
    inverted = swap(inverse(gram))[:, :SIDE]
    total = jnp.sum(part_ref[...], axis=0) / along
    spread[pl.ds(0, HALF, stride=2), :] = total
    spread[pl.ds(1, HALF, stride=2), :] = swap(total)
    rows = spread[:, :SIDE]
    rows = jnp.concatenate([rows, rows], axis=0)
    solved = lax.dot_general(
        inverted, rows, (((1,), (1,)), ((), ())), precision=HIGH, preferred_element_type=jnp.float32
    )
    out_ref[...] = jnp.broadcast_to(fold_halves(solved)[None], out_ref.shape)
    for pair in range(OWNERS // 2):
        left, right = unfold_halves(first_ref[2 * pair]), unfold_halves(first_ref[2 * pair + 1])
        both = jnp.concatenate([left, right], axis=0).T[:SIDE]
        new_ref[:, pair * WIDE : (pair + 1) * WIDE] = both / down


def squares(solved_ref, out_ref):
    solved = solved_ref[...]
    out_ref[...] = jnp.broadcast_to(jnp.sum(solved * solved, axis=0)[None], out_ref.shape)


def finish(solved_ref, square_ref, new_ref, scale_ref):
    total = jnp.sum(square_ref[...], axis=0)
    mask = low(total.shape)
    left = jnp.sum(jnp.where(mask, total, 0.0), axis=1, keepdims=True)
    right = jnp.sum(jnp.where(mask, 0.0, total), axis=1, keepdims=True)
    down = jnp.sqrt(jnp.concatenate([left, right], axis=0) / ROWS + 1e-06)
    shape = (SIDE, SIDE)
    eye = lax.broadcasted_iota(jnp.int32, shape, 0) == lax.broadcasted_iota(jnp.int32, shape, 1)
    scale_ref[...] = jnp.sum(jnp.where(eye, jnp.broadcast_to(down, shape), 0.0), axis=0, keepdims=True)
    for pair in range(OWNERS // 2):
        left, right = solved_ref[2 * pair], solved_ref[2 * pair + 1]
        upper = jnp.where(mask, left, swap(right))
        lower = jnp.where(mask, swap(left), right)
        both = jnp.concatenate([upper, lower], axis=0)
        new_ref[:, pair * WIDE : (pair + 1) * WIDE] = both / down


def struct(*shape):
    return jax.ShapeDtypeStruct(shape, jnp.float32)


def exchange(x, axis):
    return lax.all_to_all(x, axis, 0, 0, tiled=True)


def whole(*shape):
    return pl.BlockSpec(shape, lambda slot, *_: (0,) * len(shape))


def shards(blocks, coords, counts, factor_b, factor_c):
    second = factor_b.T
    spread, gram_b = pl.pallas_call(
        prepare, out_shape=(struct(OWNERS, HALF, WIDE), struct(SIDE, WIDE)), compiler_params=LIMIT
    )(second, factor_c)
    asked = exchange(jnp.broadcast_to(coords[None, :, 2], (PEERS, SLOTS)), "rows")
    held = exchange(spread, "slab")
    answers = pl.pallas_call(
        answer,
        grid_spec=pltpu.PrefetchScalarGridSpec(
            num_scalar_prefetch=1,
            grid=(1,),
            in_specs=[whole(OWNERS, HALF, WIDE), whole(SIDE, WIDE)],
            out_specs=whole(PEERS, SLOTS * HALF + SIDE, WIDE),
        ),
        out_shape=struct(PEERS, SLOTS * HALF + SIDE, WIDE),
        compiler_params=LIMIT,
    )(asked, held, gram_b)
    third = exchange(answers, "rows")
    folded, part_a, inverse_a, gram_c = pl.pallas_call(
        fold,
        grid_spec=pltpu.PrefetchScalarGridSpec(
            num_scalar_prefetch=2,
            grid=(SLOTS,),
            in_specs=[
                pl.BlockSpec((1, SIDE, SIDE * SIDE), lambda slot, *_: (slot, 0, 0)),
                whole(PEERS, SLOTS * HALF + SIDE, WIDE),
                whole(SIDE, GROUP),
            ],
            out_specs=[
                pl.BlockSpec((1, HALF, SIDE, WIDE), lambda slot, *_: (slot, 0, 0, 0)),
                whole(OWNERS, HALF, WIDE),
                whole(WIDE, WIDE),
                whole(SIDE, WIDE),
            ],
            scratch_shapes=[pltpu.VMEM((WIDE, WIDE), jnp.float32)],
        ),
        out_shape=(
            struct(SLOTS, HALF, SIDE, WIDE),
            struct(OWNERS, HALF, WIDE),
            struct(WIDE, WIDE),
            struct(SIDE, WIDE),
        ),
        compiler_params=LIMIT,
    )(coords, counts, blocks, third, second)
    solved_a = pl.pallas_call(solve_first, out_shape=struct(OWNERS, HALF, WIDE), compiler_params=LIMIT)(
        exchange(part_a, "slab"), inverse_a
    )
    group_a = exchange(solved_a, "slab")
    part_b, square_a = pl.pallas_call(
        contract,
        grid_spec=pltpu.PrefetchScalarGridSpec(
            num_scalar_prefetch=2,
            grid=(SLOTS,),
            in_specs=[
                pl.BlockSpec((1, HALF, SIDE, WIDE), lambda slot, *_: (slot, 0, 0, 0)),
                whole(OWNERS, HALF, WIDE),
            ],
            out_specs=[whole(OWNERS, HALF, WIDE), whole(PEERS, HALF, WIDE)],
        ),
        out_shape=(struct(OWNERS, HALF, WIDE), struct(PEERS, HALF, WIDE)),
        compiler_params=LIMIT,
    )(coords, counts, folded, group_a)
    square_a = exchange(square_a, "rows")
    solved_b, new_a = pl.pallas_call(
        solve_second,
        out_shape=(struct(OWNERS, HALF, WIDE), struct(SIDE, GROUP)),
        scratch_shapes=[pltpu.VMEM((SIDE, WIDE), jnp.float32)],
        compiler_params=LIMIT,
    )(exchange(part_b, "slab"), square_a, gram_c, group_a)
    group_b = exchange(solved_b, "slab")
    square_b = pl.pallas_call(squares, out_shape=struct(PEERS, HALF, WIDE), compiler_params=LIMIT)(group_b)
    new_b, scale_b = pl.pallas_call(
        finish, out_shape=(struct(SIDE, GROUP), struct(1, SIDE)), compiler_params=LIMIT
    )(group_b, exchange(square_b, "rows"))
    return (new_a.T, new_b.T, scale_b.reshape(SIDE))


def solution(mesh):
    in_specs = (
        P(("slab", "rows"), None, None),
        P(("slab", "rows"), None),
        P(("slab", "rows")),
        P("rows", None),
        P(("slab", "rows"), None),
    )
    out_specs = (P("rows", None), P("rows", None), P())
    return jax.shard_map(shards, mesh=mesh, in_specs=in_specs, out_specs=out_specs, check_vma=False)
```

```python
import jax
import jax.numpy as jnp
from jax import lax
from jax.experimental import pallas as pl
from jax.experimental.pallas import tpu as pltpu
from jax.sharding import PartitionSpec as P

SIDE = 64
HALF = 32
WIDE = 128
TILE = 8
SLOTS = 6
PEERS = 8
OWNERS = 32
GROUP = 2048
ROWS = 16384
HIGH = lax.Precision.HIGHEST
LIMIT = pltpu.CompilerParams(vmem_limit_bytes=24 * 1024 * 1024)
LARGE = pltpu.CompilerParams(vmem_limit_bytes=48 * 1024 * 1024)


def low(shape):
    return lax.broadcasted_iota(jnp.int32, shape, len(shape) - 1) < SIDE


def swap(x):
    return pltpu.roll(x, SIDE, 1)


def unfold_halves(packed):
    mask, other = low(packed.shape), swap(packed)
    return jnp.concatenate([jnp.where(mask, packed, other), jnp.where(mask, other, packed)], axis=0)


def fold_halves(rows):
    return jnp.where(low((HALF, WIDE)), rows[:HALF], rows[HALF:])


def product(left, right, left_dim=1, right_dim=0):
    return lax.dot_general(
        left,
        right,
        (((left_dim,), (right_dim,)), ((), ())),
        precision=HIGH,
        preferred_element_type=jnp.float32,
    )


def gram_packed(packed):
    both = product(packed, packed, 0, 0)
    total = both[:SIDE] + swap(both[SIDE:])
    return fold_halves(jnp.where(low(total.shape), total, swap(total)))


def inverse(gram):
    shape = gram.shape
    row = lax.broadcasted_iota(jnp.int32, shape, 0)
    lane = lax.broadcasted_iota(jnp.int32, shape, 1)
    work = jnp.where(lane < SIDE, gram, jnp.where(lane - SIDE == row, 1.0, 0.0))
    for k in range(SIDE):
        line = work[k : k + 1, :] / work[k : k + 1, k : k + 1]
        column = work[:, k : k + 1]
        work = jnp.where(row == k, line, work - column * line)
    zero = jnp.zeros_like(work)
    mask = lane < SIDE
    return jnp.concatenate([jnp.where(mask, swap(work), zero), jnp.where(mask, zero, work)], axis=0)


def pick(meta, at):
    lane = lax.broadcasted_iota(jnp.int32, meta.shape, 1)
    hit = (meta == (lane - at).astype(jnp.float32)) & (lane >= at) & (lane < at + OWNERS)
    return jnp.where(hit, 1.0, 0.0)


def lines(ref):
    return ref[...].reshape(OWNERS * TILE, WIDE)


def places(ref):
    return ref[:, TILE:, :].reshape(OWNERS * TILE, WIDE)


def prepare(place_ref, count_ref, third_ref, second_ref, out_ref, tile, arrived):
    own = lax.axis_index("slab")
    copy = pltpu.make_async_copy(
        second_ref.at[:, pl.ds(pl.multiple_of(own // 2 * WIDE, WIDE), WIDE)], tile, arrived
    )
    copy.start()
    third = third_ref[...]
    twice = jnp.concatenate([third, third], axis=1)
    out_ref[:, 0, :] = fold_halves(twice)
    out_ref[:, 2, :] = fold_halves(product(third, twice, 0, 0))
    out_ref[:, 3:TILE, :] = jnp.zeros((OWNERS, TILE - 3, WIDE), jnp.float32)
    row = lax.broadcasted_iota(jnp.int32, (TILE, WIDE), 0)
    lane = lax.broadcasted_iota(jnp.int32, (TILE, WIDE), 1)
    meta = jnp.full((TILE, WIDE), -1, jnp.int32)
    for slot in range(SLOTS):
        which = place_ref[slot, 2]
        value = jnp.where(
            lane < OWNERS,
            place_ref[slot, 0] % OWNERS,
            jnp.where(lane < 2 * OWNERS, place_ref[slot, 1] % OWNERS, which % PEERS * OWNERS + which // PEERS),
        )
        meta = jnp.where((row == slot) & (slot < count_ref[0]), value, meta)
    out_ref[:, TILE:, :] = jnp.broadcast_to(meta.astype(jnp.float32)[None], (OWNERS, TILE, WIDE))
    copy.wait()
    second = tile[...]
    share = lax.broadcasted_iota(jnp.int32, second.shape, 1) // SIDE == own % 2
    out_ref[:, 1, :] = fold_halves(
        product(jnp.where(share, second, 0.0), jnp.concatenate([second, second], axis=0), 1, 1)
    )


def relay(first_ref, out_ref):
    out_ref[:, :HALF, :] = jnp.broadcast_to(first_ref[:, 0, :][None], (PEERS, HALF, WIDE))
    grams = jnp.sum(first_ref[:, :TILE, :], axis=0)
    out_ref[:, HALF:, :] = jnp.broadcast_to(grams[None], (PEERS, TILE, WIDE))


def answer(meta_ref, held_ref, out_ref):
    wanted = places(meta_ref)[:, 2 * OWNERS : 2 * OWNERS + 1]
    lane = lax.broadcasted_iota(jnp.int32, (OWNERS * TILE, PEERS * OWNERS), 1).astype(jnp.float32)
    held = held_ref[:, :HALF, :].reshape(PEERS * OWNERS, WIDE)
    found = product(jnp.where(wanted == lane, 1.0, 0.0), held)
    grams = jnp.sum(held_ref[:, HALF:, :], axis=0)
    out_ref[...] = found.reshape(OWNERS, TILE, WIDE)
    out_ref[:, SLOTS, :] = jnp.broadcast_to(grams[1:2], (OWNERS, WIDE))
    out_ref[:, SLOTS + 1, :] = jnp.broadcast_to(grams[2:3], (OWNERS, WIDE))


def split(x):
    high = x.astype(jnp.bfloat16)
    return high, (x - high.astype(jnp.float32)).astype(jnp.bfloat16)


def fold(
    place_ref,
    count_ref,
    blocks_ref,
    third_ref,
    second_ref,
    folded_ref,
    out_ref,
    held,
    made,
    tiles,
    third_rows,
    terms,
    turned,
    held_sem,
    made_sem,
    tile_sem,
):
    count = count_ref[0]

    def load(slot):
        return pltpu.make_async_copy(blocks_ref.at[slot], held.at[slot], held_sem.at[slot])

    def load_tile(slot):
        start = pl.multiple_of(place_ref[slot, 1] % OWNERS // 2 * WIDE, WIDE)
        return pltpu.make_async_copy(second_ref.at[:, pl.ds(start, WIDE)], tiles.at[slot], tile_sem.at[slot])

    def store(slot):
        return pltpu.make_async_copy(made.at[slot], folded_ref.at[slot], made_sem.at[slot])

    for slot in range(SLOTS):

        @pl.when(slot < count)
        def _():
            load_tile(slot).start()
            load(slot).start()

    for slot in range(SLOTS):
        third_rows[slot] = third_ref[:, slot, :]
    terms[...] = jnp.zeros_like(terms)

    @pl.loop(0, count)
    def _(slot):
        packed = third_rows[slot]
        mask, other = low(packed.shape), swap(packed)
        zero = jnp.zeros_like(packed)
        twin = jnp.concatenate(
            [
                jnp.where(mask, packed, zero),
                jnp.where(mask, other, zero),
                jnp.where(mask, zero, other),
                jnp.where(mask, zero, packed),
            ],
            axis=0,
        )
        high, rest = split(twin)
        weights = jnp.concatenate([high, rest], axis=1)
        weights = jnp.concatenate([weights, weights], axis=0)
        load_tile(slot).wait()
        tile = tiles[slot]
        turned[...] = jnp.concatenate([tile, tile], axis=0).T
        start = place_ref[slot, 1] % 2 * SIDE
        pairs = jnp.where(
            mask, turned[pl.ds(start, HALF, stride=2), :], turned[pl.ds(start + 1, HALF, stride=2), :]
        )
        load(slot).wait()
        total = jnp.zeros((SIDE, WIDE), jnp.float32)
        step = 8
        for at in range(0, HALF, step):
            rows = jnp.concatenate(
                [held[slot, :, (at + n) * WIDE : (at + n + 1) * WIDE] for n in range(step)], axis=0
            )
            high, rest = split(rows)
            rows = jnp.concatenate([high, rest], axis=1)
            both = jnp.dot(rows, weights, preferred_element_type=jnp.float32)
            both = both[:, :WIDE] + both[:, WIDE:]
            for n in range(step):
                piece = both[n * SIDE : (n + 1) * SIDE]
                made[slot, at + n] = piece
                total += piece * pairs[at + n : at + n + 1, :]
        store(slot).start()
        terms[slot] = fold_halves(total + swap(total))

    for k in range(TILE):
        out_ref[:, k, :] = terms[k]

    for slot in range(SLOTS):

        @pl.when(slot < count)
        def _():
            store(slot).wait()


def invert_first(third_ref, out_ref):
    out_ref[...] = inverse(unfold_halves(third_ref[:, SLOTS, :] * third_ref[:, SLOTS + 1, :]))


def solve_first(part_ref, meta_ref, inverse_ref, spread_ref):
    total = product(pick(places(meta_ref), 0), lines(part_ref), 0, 0)[:OWNERS]
    spread_ref[...] = jnp.broadcast_to(product(total, inverse_ref[...])[None], spread_ref.shape)


def gram_first(first_ref, out_ref):
    out_ref[...] = jnp.broadcast_to(gram_packed(first_ref[...])[None], out_ref.shape)


def contract(place_ref, count_ref, folded_ref, first_ref, out_ref, terms, spaced):
    slot = pl.program_id(0)

    @pl.when(slot == 0)
    def _():
        terms[...] = jnp.zeros_like(terms)

    @pl.when(slot < count_ref[0])
    def _():
        first = first_ref[pl.ds(place_ref[slot, 0] % OWNERS, HALF, stride=OWNERS), :]
        term = jnp.sum(folded_ref[0] * unfold_halves(first)[None], axis=1)
        spaced[pl.ds(0, HALF, stride=2), :] = term
        spaced[pl.ds(1, HALF, stride=2), :] = swap(term)
        terms[slot] = jnp.where(low(term.shape), spaced[:HALF, :], swap(spaced[HALF:, :]))

    @pl.when(slot == SLOTS - 1)
    def _():
        for k in range(TILE):
            out_ref[:, k, :] = terms[k]


def invert_second(square_ref, third_ref, out_ref, scale_ref):
    square = unfold_halves(jnp.sum(square_ref[...], axis=0))
    shape = square.shape
    row = lax.broadcasted_iota(jnp.int32, shape, 0)
    lane = lax.broadcasted_iota(jnp.int32, shape, 1)
    means = jnp.where(row == lane % SIDE, square, 0.0) / ROWS
    along = jnp.sqrt(jnp.sum(means, axis=0, keepdims=True) + 1e-06)
    down = jnp.sqrt(jnp.sum(jnp.where(lane < SIDE, means, 0.0), axis=1, keepdims=True) + 1e-06)
    scale_ref[...] = along
    out_ref[...] = inverse(square / along / down * unfold_halves(third_ref[:, SLOTS + 1, :]))


def solve_second(part_ref, meta_ref, inverse_ref, scale_ref, spread_ref):
    total = product(pick(places(meta_ref), OWNERS), lines(part_ref), 0, 0)[OWNERS : 2 * OWNERS]
    solved = product(total / scale_ref[...], inverse_ref[...])
    spread_ref[...] = jnp.broadcast_to(solved[None], spread_ref.shape)


def turn(solved_ref, scale, out_ref):
    mask = low((HALF, WIDE))
    half = OWNERS // 2
    for pair in range(half // 2):
        parts = []
        for block in (2 * pair, 2 * pair + 1):
            left = solved_ref[:, block, :] / scale
            right = solved_ref[:, block + half, :] / scale
            parts += [jnp.where(mask, left, swap(right)), jnp.where(mask, swap(left), right)]
        both = jnp.concatenate(parts, axis=0).T
        out_ref[:, pair * WIDE : (pair + 1) * WIDE] = both[:SIDE]
        out_ref[:, GROUP // 2 + pair * WIDE : GROUP // 2 + (pair + 1) * WIDE] = both[SIDE:]


def finish_first(solved_ref, scale_ref, new_ref):
    turn(solved_ref, scale_ref[...], new_ref)


def squares(solved_ref, out_ref):
    solved = solved_ref[...].reshape(OWNERS * HALF, WIDE)
    total = jnp.sum(solved * solved, axis=0, keepdims=True)
    out_ref[...] = jnp.broadcast_to(total[None], out_ref.shape)


def finish_second(solved_ref, square_ref, new_ref, scale_ref):
    total = jnp.sum(square_ref[:, 0, :], axis=0, keepdims=True)
    scale = jnp.sqrt((total + swap(total)) / ROWS + 1e-06)
    scale_ref[...] = scale[:, :SIDE]
    turn(solved_ref, scale, new_ref)


def struct(*shape):
    return jax.ShapeDtypeStruct(shape, jnp.float32)


def exchange(x, axis):
    return lax.all_to_all(x, axis, 0, 0, tiled=True)


def whole(*shape):
    return pl.BlockSpec(shape, lambda *_: (0,) * len(shape))


def call(body, *outs):
    return pl.pallas_call(body, out_shape=outs if len(outs) > 1 else outs[0], compiler_params=LIMIT)


def shards(blocks, coords, counts, factor_b, factor_c):
    second = factor_b.T
    scalars = pl.BlockSpec(memory_space=pltpu.SMEM)
    local = pl.BlockSpec(memory_space=pltpu.VMEM)
    apart = pl.BlockSpec(memory_space=pltpu.HBM)
    small = (OWNERS, TILE, WIDE)
    full = (OWNERS, HALF, WIDE)
    opening = pl.pallas_call(
        prepare,
        in_specs=[scalars, scalars, local, apart],
        out_specs=local,
        out_shape=struct(OWNERS, 2 * TILE, WIDE),
        scratch_shapes=[pltpu.VMEM((SIDE, WIDE), jnp.float32), pltpu.SemaphoreType.DMA],
        compiler_params=LIMIT,
    )(coords, counts, factor_c, second)
    meta = exchange(opening, "slab")
    held = exchange(call(relay, struct(PEERS, HALF + TILE, WIDE))(meta), "rows")
    third = exchange(call(answer, struct(*small))(meta, held), "slab")
    folded, part_a = pl.pallas_call(
        fold,
        in_specs=[scalars, scalars, apart, local, apart],
        out_specs=[apart, local],
        out_shape=(struct(SLOTS, HALF, SIDE, WIDE), struct(*small)),
        scratch_shapes=[
            pltpu.VMEM((SLOTS, SIDE, SIDE * SIDE), jnp.float32),
            pltpu.VMEM((SLOTS, HALF, SIDE, WIDE), jnp.float32),
            pltpu.VMEM((SLOTS, SIDE, WIDE), jnp.float32),
            pltpu.VMEM((SLOTS, HALF, WIDE), jnp.float32),
            pltpu.VMEM((TILE, HALF, WIDE), jnp.float32),
            pltpu.VMEM((WIDE, WIDE), jnp.float32),
            pltpu.SemaphoreType.DMA((SLOTS,)),
            pltpu.SemaphoreType.DMA((SLOTS,)),
            pltpu.SemaphoreType.DMA((SLOTS,)),
        ],
        compiler_params=LARGE,
    )(coords, counts, blocks, third, second)
    part_a = exchange(part_a, "slab")
    inverse_a = call(invert_first, struct(WIDE, WIDE))(third)
    whole_a = exchange(call(solve_first, struct(*full))(part_a, meta, inverse_a), "slab")
    first = whole_a.reshape(OWNERS * HALF, WIDE)
    square_a = exchange(call(gram_first, struct(PEERS, HALF, WIDE))(first), "rows")
    part_b = pl.pallas_call(
        contract,
        grid_spec=pltpu.PrefetchScalarGridSpec(
            num_scalar_prefetch=2,
            grid=(SLOTS,),
            in_specs=[
                pl.BlockSpec((1, HALF, SIDE, WIDE), lambda slot, *_: (slot, 0, 0, 0)),
                whole(OWNERS * HALF, WIDE),
            ],
            out_specs=whole(*small),
            scratch_shapes=[
                pltpu.VMEM((TILE, HALF, WIDE), jnp.float32),
                pltpu.VMEM((SIDE, WIDE), jnp.float32),
            ],
        ),
        out_shape=struct(*small),
        compiler_params=LARGE,
    )(coords, counts, folded, first)
    part_b = exchange(part_b, "slab")
    inverse_b, scale_a = call(invert_second, struct(WIDE, WIDE), struct(1, WIDE))(square_a, third)
    new_a = call(finish_first, struct(SIDE, GROUP))(whole_a, scale_a)
    inverse_b, new_a = lax.optimization_barrier((inverse_b, new_a))
    spread_b = call(solve_second, struct(*full))(part_b, meta, inverse_b, scale_a)
    whole_b = exchange(spread_b, "slab")
    square_b = exchange(call(squares, struct(PEERS, TILE, WIDE))(whole_b), "rows")
    new_b, scale_b = call(finish_second, struct(SIDE, GROUP), struct(1, SIDE))(whole_b, square_b)
    return (new_a.T, new_b.T, scale_b.reshape(SIDE))


def solution(mesh):
    in_specs = (
        P(("slab", "rows"), None, None),
        P(("slab", "rows"), None),
        P(("slab", "rows")),
        P("rows", None),
        P(("slab", "rows"), None),
    )
    out_specs = (P("rows", None), P("rows", None), P())
    return jax.shard_map(shards, mesh=mesh, in_specs=in_specs, out_specs=out_specs, check_vma=False)
```

```python
import jax
import jax.numpy as jnp
from jax import lax
from jax.experimental import pallas as pl
from jax.experimental.pallas import tpu as pltpu
from jax.sharding import Mesh
from jax.sharding import PartitionSpec as P

SIDE = 64
HALF = 32
WIDE = 128
STEP = 8
TILE = 8
SLOTS = 6
LEAD = 2
TURNS = 4
PEERS = 8
OWNERS = 32
GROUP = 2048
ROWS = 16384
HIGH = lax.Precision.HIGHEST
SLAB = ("x", "z")
LIMIT = pltpu.CompilerParams(vmem_limit_bytes=24 * 1024 * 1024)
LARGE = pltpu.CompilerParams(vmem_limit_bytes=48 * 1024 * 1024)


def low(shape):
    return lax.broadcasted_iota(jnp.int32, shape, len(shape) - 1) < SIDE


def swap(x):
    return pltpu.roll(x, SIDE, 1)


def unfold_halves(packed):
    mask, other = low(packed.shape), swap(packed)
    return jnp.concatenate([jnp.where(mask, packed, other), jnp.where(mask, other, packed)], axis=0)


def fold_halves(rows):
    return jnp.where(low((HALF, WIDE)), rows[:HALF], rows[HALF:])


def product(left, right, left_dim=1, right_dim=0):
    return lax.dot_general(
        left,
        right,
        (((left_dim,), (right_dim,)), ((), ())),
        precision=HIGH,
        preferred_element_type=jnp.float32,
    )


def gram_packed(packed):
    both = product(packed, packed, 0, 0)
    total = both[:SIDE] + swap(both[SIDE:])
    return fold_halves(jnp.where(low(total.shape), total, swap(total)))


def inverse(gram):
    shape = gram.shape
    row = lax.broadcasted_iota(jnp.int32, shape, 0)
    lane = lax.broadcasted_iota(jnp.int32, shape, 1)
    work = jnp.where(lane < SIDE, gram, jnp.where(lane - SIDE == row, 1.0, 0.0))
    for k in range(SIDE):
        line = work[k : k + 1, :] / work[k : k + 1, k : k + 1]
        column = work[:, k : k + 1]
        work = jnp.where(row == k, line, work - column * line)
    zero = jnp.zeros_like(work)
    mask = lane < SIDE
    return jnp.concatenate([jnp.where(mask, swap(work), zero), jnp.where(mask, zero, work)], axis=0)


def held(shape):
    return lax.broadcasted_iota(jnp.int32, shape, 0) % TILE >= LEAD


def pick(meta, at):
    lane = lax.broadcasted_iota(jnp.int32, meta.shape, 1)
    hit = (meta == (lane - at).astype(jnp.float32)) & (lane >= at) & (lane < at + OWNERS) & held(meta.shape)
    return jnp.where(hit, 1.0, 0.0)


def lines(ref):
    return ref[...].reshape(OWNERS * TILE, WIDE)


def prepare(given_ref, out_ref, place_ref):
    third = given_ref[:SIDE, :]
    twice = jnp.concatenate([third, third], axis=1)
    piece, gram = fold_halves(twice), fold_halves(product(third, twice, 0, 0))
    given = given_ref[SIDE:, :].astype(jnp.int32)
    place_ref[...] = given
    row = lax.broadcasted_iota(jnp.int32, given.shape, 0)
    lane = lax.broadcasted_iota(jnp.int32, given.shape, 1)
    first, second, third = (
        jnp.sum(jnp.where(lane == row - LEAD, given[n : n + 1, :], 0), axis=1, keepdims=True) for n in range(3)
    )
    row = lax.broadcasted_iota(jnp.int32, (TILE, WIDE), 0)
    lane = lax.broadcasted_iota(jnp.int32, (TILE, WIDE), 1)
    meta = jnp.where(
        lane < OWNERS,
        first % OWNERS,
        jnp.where(lane < 2 * OWNERS, second % OWNERS, third % PEERS * OWNERS + third // PEERS),
    )
    meta = jnp.where((row >= LEAD) & (row - LEAD < given[3:4, 0:1]), meta, -1)
    out_ref[...] = jnp.broadcast_to(meta.astype(jnp.float32)[None], out_ref.shape)
    out_ref[:, 0, :] = piece
    out_ref[:, 1, :] = gram


def arrange(second_ref, gram_ref, pairs_ref, turned):
    second = second_ref[...]
    gram_ref[...] = fold_halves(product(second, jnp.concatenate([second, second], axis=0), 1, 1))
    mask = low((HALF, WIDE))
    for pair in range(OWNERS // 2):
        tile = second[:, pair * WIDE : (pair + 1) * WIDE]
        turned[pair % 2] = jnp.concatenate([tile, tile], axis=0).T
        for n in range(2):
            even = turned[pair % 2, pl.ds(n * SIDE, HALF, stride=2), :]
            odd = turned[pair % 2, pl.ds(n * SIDE + 1, HALF, stride=2), :]
            pairs_ref[2 * pair + n] = jnp.where(mask, even, odd)


def relay(first_ref, gram_ref, out_ref):
    out_ref[:, :HALF, :] = jnp.broadcast_to(first_ref[:, 0, :][None], (PEERS, HALF, WIDE))
    second = gram_ref[pl.ds(lax.axis_index(SLAB), 1), :]
    third = jnp.sum(first_ref[:, 1, :], axis=0, keepdims=True)
    row = lax.broadcasted_iota(jnp.int32, (TILE, WIDE), 0)
    grams = jnp.where(row == 0, second, jnp.where(row == 1, third, 0.0))
    out_ref[:, HALF:, :] = jnp.broadcast_to(grams[None], (PEERS, TILE, WIDE))


def answer(meta_ref, held_ref, out_ref):
    wanted = lines(meta_ref)[:, 2 * OWNERS : 2 * OWNERS + 1]
    shape = (OWNERS * TILE, PEERS * OWNERS)
    lane = lax.broadcasted_iota(jnp.int32, shape, 1).astype(jnp.float32)
    stock = held_ref[:, :HALF, :].reshape(PEERS * OWNERS, WIDE)
    found = product(jnp.where((wanted == lane) & held(shape), 1.0, 0.0), stock)
    grams = jnp.sum(held_ref[:, HALF:, :], axis=0)
    out_ref[...] = found.reshape(OWNERS, TILE, WIDE)
    out_ref[:, 0, :] = jnp.broadcast_to(grams[0:1], (OWNERS, WIDE))
    out_ref[:, 1, :] = jnp.broadcast_to(grams[1:2], (OWNERS, WIDE))


def split(x):
    high = x.astype(jnp.bfloat16)
    return high, (x - high.astype(jnp.float32)).astype(jnp.bfloat16)


def fold(
    place_ref,
    blocks_ref,
    third_ref,
    pairs_ref,
    folded_ref,
    out_ref,
    held,
    made,
    weights,
    terms,
    held_sem,
    made_sem,
):
    count = place_ref[3, 0]

    def load(slot):
        return pltpu.make_async_copy(blocks_ref.at[slot], held.at[slot], held_sem.at[slot])

    def store(slot):
        return pltpu.make_async_copy(made.at[slot], folded_ref.at[slot], made_sem.at[slot])

    for slot in range(SLOTS):

        @pl.when(slot < count)
        def _():
            load(slot).start()

    for slot in range(SLOTS):
        packed = third_ref[:, slot + LEAD, :]
        mask, other = low(packed.shape), swap(packed)
        zero = jnp.zeros_like(packed)
        twin = jnp.concatenate(
            [
                jnp.where(mask, packed, zero),
                jnp.where(mask, other, zero),
                jnp.where(mask, zero, other),
                jnp.where(mask, zero, packed),
            ],
            axis=0,
        )
        high, rest = split(twin)
        twin = jnp.concatenate([high, rest], axis=1)
        weights[slot] = jnp.concatenate([twin, twin], axis=0)
    terms[...] = jnp.zeros_like(terms)

    @pl.loop(0, count)
    def _(slot):
        pairs = pairs_ref[place_ref[1, slot] % OWNERS]
        load(slot).wait()
        total = jnp.zeros((SIDE, WIDE), jnp.float32)
        for at in range(0, HALF, STEP):
            rows = jnp.concatenate(
                [held[slot, :, (at + n) * WIDE : (at + n + 1) * WIDE] for n in range(STEP)], axis=0
            )
            high, rest = split(rows)
            rows = jnp.concatenate([high, rest], axis=1)
            both = jnp.dot(rows, weights[slot], preferred_element_type=jnp.float32)
            both = both[:, :WIDE] + both[:, WIDE:]
            for n in range(STEP):
                piece = both[n * SIDE : (n + 1) * SIDE]
                made[slot, at + n] = piece
                total += piece * pairs[at + n : at + n + 1, :]
        store(slot).start()
        terms[slot + LEAD] = fold_halves(total + swap(total))

    for k in range(TILE):
        out_ref[:, k, :] = terms[k]

    for slot in range(SLOTS):

        @pl.when(slot < count)
        def _():
            store(slot).wait()


def invert_first(third_ref, out_ref):
    out_ref[...] = inverse(unfold_halves(third_ref[:, 0, :] * third_ref[:, 1, :]))


def solve_first(part_ref, meta_ref, inverse_ref, out_ref, solved_ref):
    chosen = pick(lines(meta_ref), 0)
    solved = product(product(chosen, lines(part_ref), 0, 0), inverse_ref[...])
    out_ref[...] = product(chosen, solved).reshape(OWNERS, TILE, WIDE)
    solved = solved[:OWNERS]
    out_ref[:, 0, :] = gram_packed(solved)
    solved_ref[...] = solved


def share_gram(first_ref, out_ref):
    total = jnp.sum(first_ref[:, 0, :], axis=0, keepdims=True)
    out_ref[...] = jnp.broadcast_to(total[None], out_ref.shape)


def contract(place_ref, folded_ref, first_ref, out_ref, held, first_rows, terms, spaced, held_sem):
    count = place_ref[3, 0]

    def load(slot):
        return pltpu.make_async_copy(folded_ref.at[slot], held.at[slot], held_sem.at[slot])

    for slot in range(SLOTS):

        @pl.when(slot < count)
        def _():
            load(slot).start()

    terms[...] = jnp.zeros_like(terms)
    for slot in range(SLOTS):
        first_rows[slot] = first_ref[:, slot + LEAD, :]

    @pl.loop(0, count)
    def _(slot):
        first = unfold_halves(first_rows[slot])
        load(slot).wait()
        term = jnp.sum(held[slot] * first[None], axis=1)
        spaced[pl.ds(0, HALF, stride=2), :] = term
        spaced[pl.ds(1, HALF, stride=2), :] = swap(term)
        terms[slot + LEAD] = jnp.where(low(term.shape), spaced[:HALF, :], swap(spaced[HALF:, :]))

    for k in range(TILE):
        out_ref[:, k, :] = terms[k]


def insert(part_ref, square_ref, out_ref):
    out_ref[...] = part_ref[...]
    total = jnp.sum(square_ref[:, 0, :], axis=0, keepdims=True)
    out_ref[:, 0, :] = jnp.broadcast_to(total, (OWNERS, WIDE))


def sum_second(part_ref, meta_ref, solved_ref, out_ref):
    total = product(pick(lines(meta_ref), OWNERS), lines(part_ref), 0, 0)[OWNERS : 2 * OWNERS]
    both = jnp.concatenate([total, solved_ref[...]], axis=0)
    out_ref[...] = jnp.broadcast_to(both[None], out_ref.shape)


def invert_second(part_ref, third_ref, out_ref, scale_ref):
    square = unfold_halves(part_ref[:, 0, :])
    shape = square.shape
    row = lax.broadcasted_iota(jnp.int32, shape, 0)
    lane = lax.broadcasted_iota(jnp.int32, shape, 1)
    means = jnp.where(row == lane % SIDE, square, 0.0) / ROWS
    along = jnp.sqrt(jnp.sum(means, axis=0, keepdims=True) + 1e-06)
    down = jnp.sqrt(jnp.sum(jnp.where(lane < SIDE, means, 0.0), axis=1, keepdims=True) + 1e-06)
    scale_ref[...] = along
    out_ref[...] = inverse(square / along / down * unfold_halves(third_ref[:, 1, :]))


def solve_second(near_ref, inverse_ref, scale_ref, out_ref, square_ref):
    near = near_ref[...] / scale_ref[...]
    solved = product(near[:, :HALF].reshape(PEERS * HALF, WIDE), inverse_ref[...])
    out_ref[:, :HALF, :] = solved.reshape(PEERS, HALF, WIDE)
    out_ref[:, HALF:, :] = near[:, HALF:]
    total = jnp.sum(solved * solved, axis=0, keepdims=True)
    square_ref[...] = jnp.broadcast_to(total[None], square_ref.shape)


def turn(solved_ref, out_ref):
    mask = low((HALF, WIDE))
    half = OWNERS // 2
    for pair in range(half // 2):
        parts = []
        for block in (2 * pair, 2 * pair + 1):
            left, right = solved_ref[:, block, :], solved_ref[:, block + half, :]
            parts += [jnp.where(mask, left, swap(right)), jnp.where(mask, swap(left), right)]
        both = jnp.concatenate(parts, axis=0).T
        out_ref[:, pair * WIDE : (pair + 1) * WIDE] = both[:SIDE]
        out_ref[:, GROUP // 2 + pair * WIDE : GROUP // 2 + (pair + 1) * WIDE] = both[SIDE:]


def collect(parts, which, scale, out_ref):
    own = lax.axis_index("x")
    for step, part in enumerate(parts):
        rows = part[:, which * HALF : (which + 1) * HALF, :]
        out_ref[pl.ds((own + TURNS - step) % TURNS * PEERS, PEERS)] = rows if scale is None else rows / scale


def finish_first(own_ref, one_ref, two_ref, three_ref, new_ref, solved):
    collect((own_ref, one_ref, two_ref, three_ref), 1, None, solved)
    turn(solved, new_ref)


def finish_second(own_ref, one_ref, two_ref, three_ref, square_ref, new_ref, scale_ref, solved):
    total = jnp.sum(square_ref[:, 0, :], axis=0, keepdims=True)
    scale = jnp.sqrt((total + swap(total)) / ROWS + 1e-06)
    scale_ref[...] = scale[:, :SIDE]
    collect((own_ref, one_ref, two_ref, three_ref), 0, scale, solved)
    turn(solved, new_ref)


def struct(*shape):
    return jax.ShapeDtypeStruct(shape, jnp.float32)


def exchange(x, axis):
    return lax.all_to_all(x, axis, 0, 0, tiled=True)


def call(body, *outs):
    return pl.pallas_call(body, out_shape=outs if len(outs) > 1 else outs[0], compiler_params=LIMIT)


def shards(blocks, coords, counts, factor_b, factor_c):
    scalars = pl.BlockSpec(memory_space=pltpu.SMEM)
    local = pl.BlockSpec(memory_space=pltpu.VMEM)
    apart = pl.BlockSpec(memory_space=pltpu.HBM)
    small = (OWNERS, TILE, WIDE)
    full = (OWNERS, HALF, WIDE)
    given = jnp.pad(coords, ((0, SIDE - SLOTS), (SIDE, TILE - 3))).T.astype(jnp.float32)
    row = lax.broadcasted_iota(jnp.int32, given.shape, 0)
    given = jnp.where(row < SIDE, jnp.pad(factor_c, ((0, TILE), (0, 0))), given)
    given = jnp.where(row < SIDE + 3, given, counts.astype(jnp.float32)[:, None])
    opening, place = pl.pallas_call(
        prepare,
        out_shape=(struct(*small), jax.ShapeDtypeStruct((TILE, SIDE), jnp.int32)),
        compiler_params=LIMIT,
    )(given)
    meta = exchange(opening, SLAB)
    gram_b, pairs = pl.pallas_call(
        arrange,
        out_shape=(struct(HALF, WIDE), struct(*full)),
        scratch_shapes=[pltpu.VMEM((2, WIDE, WIDE), jnp.float32)],
        compiler_params=LIMIT,
    )(factor_b.T)
    held = exchange(call(relay, struct(PEERS, HALF + TILE, WIDE))(meta, gram_b), "rows")
    third = exchange(call(answer, struct(*small))(meta, held), SLAB)
    folded, part_a = pl.pallas_call(
        fold,
        in_specs=[scalars, apart, local, local],
        out_specs=[apart, local],
        out_shape=(struct(SLOTS, HALF, SIDE, WIDE), struct(*small)),
        scratch_shapes=[
            pltpu.VMEM((SLOTS, SIDE, SIDE * SIDE), jnp.float32),
            pltpu.VMEM((SLOTS, HALF, SIDE, WIDE), jnp.float32),
            pltpu.VMEM((SLOTS, 2 * WIDE, 2 * WIDE), jnp.bfloat16),
            pltpu.VMEM((TILE, HALF, WIDE), jnp.float32),
            pltpu.SemaphoreType.DMA((SLOTS,)),
            pltpu.SemaphoreType.DMA((SLOTS,)),
        ],
        compiler_params=LARGE,
    )(place, blocks, third, pairs)
    part_a = exchange(part_a, SLAB)
    inverse_a = call(invert_first, struct(WIDE, WIDE))(third)
    answer_a, solved_a = call(solve_first, struct(*small), struct(HALF, WIDE))(part_a, meta, inverse_a)
    first = exchange(answer_a, SLAB)
    square_a = exchange(call(share_gram, struct(PEERS, TILE, WIDE))(first), "rows")
    part_b = pl.pallas_call(
        contract,
        in_specs=[scalars, apart, local],
        out_specs=local,
        out_shape=struct(*small),
        scratch_shapes=[
            pltpu.VMEM((SLOTS, HALF, SIDE, WIDE), jnp.float32),
            pltpu.VMEM((SLOTS, HALF, WIDE), jnp.float32),
            pltpu.VMEM((TILE, HALF, WIDE), jnp.float32),
            pltpu.VMEM((SIDE, WIDE), jnp.float32),
            pltpu.SemaphoreType.DMA((SLOTS,)),
        ],
        compiler_params=LARGE,
    )(place, folded, first)
    part_b = exchange(call(insert, struct(*small))(part_b, square_a), SLAB)
    near = exchange(call(sum_second, struct(PEERS, SIDE, WIDE))(part_b, meta, solved_a), "z")
    inverse_b, scale_a = call(invert_second, struct(WIDE, WIDE), struct(1, WIDE))(part_b, third)
    near, square_b = call(solve_second, struct(PEERS, SIDE, WIDE), struct(*small))(near, inverse_b, scale_a)
    parts = [near] + [
        lax.ppermute(near, "x", [(n, (n + step) % TURNS) for n in range(TURNS)]) for step in range(1, TURNS)
    ]
    square_b = exchange(square_b, ("x", "rows"))
    scratch = [pltpu.VMEM(full, jnp.float32)]
    new_a = pl.pallas_call(
        finish_first, out_shape=struct(SIDE, GROUP), scratch_shapes=scratch, compiler_params=LIMIT
    )(*parts)
    new_b, scale_b = pl.pallas_call(
        finish_second,
        out_shape=(struct(SIDE, GROUP), struct(1, SIDE)),
        scratch_shapes=scratch,
        compiler_params=LIMIT,
    )(*parts, square_b)
    return (new_a.T, new_b.T, scale_b.reshape(SIDE))


def solution(mesh):
    mesh = Mesh(mesh.devices.reshape(TURNS, PEERS, PEERS), ("x", "z", "rows"))
    split = ("x", "z", "rows")
    in_specs = (P(split, None, None), P(split, None), P(split), P("rows", None), P(split, None))
    out_specs = (P("rows", None), P("rows", None), P())
    return jax.shard_map(shards, mesh=mesh, in_specs=in_specs, out_specs=out_specs, check_vma=False)
```

```python
import jax
import jax.numpy as jnp
from jax import lax
from jax.experimental import pallas as pl
from jax.experimental.pallas import tpu as pltpu
from jax.sharding import Mesh
from jax.sharding import PartitionSpec as P

SIDE = 64
HALF = 32
WIDE = 128
STEP = 8
BEFORE = 10
AFTER = 8
TILE = 8
SLOTS = 6
LEAD = 2
TURNS = 4
PEERS = 8
OWNERS = 32
GROUP = 2048
ROWS = 16384
HIGH = lax.Precision.HIGHEST
SLAB = ("x", "z")
LIMIT = pltpu.CompilerParams(vmem_limit_bytes=24 * 1024 * 1024)
LARGE = pltpu.CompilerParams(vmem_limit_bytes=48 * 1024 * 1024)


def low(shape):
    return lax.broadcasted_iota(jnp.int32, shape, len(shape) - 1) < SIDE


def swap(x):
    return pltpu.roll(x, SIDE, 1)


def unfold_halves(packed):
    mask, other = low(packed.shape), swap(packed)
    return jnp.concatenate([jnp.where(mask, packed, other), jnp.where(mask, other, packed)], axis=0)


def fold_halves(rows):
    return jnp.where(low((HALF, WIDE)), rows[:HALF], rows[HALF:])


def product(left, right, left_dim=1, right_dim=0):
    return lax.dot_general(
        left,
        right,
        (((left_dim,), (right_dim,)), ((), ())),
        precision=HIGH,
        preferred_element_type=jnp.float32,
    )


def gram_packed(packed):
    both = product(packed, packed, 0, 0)
    total = both[:SIDE] + swap(both[SIDE:])
    return fold_halves(jnp.where(low(total.shape), total, swap(total)))


def begin_inverse(gram):
    row = lax.broadcasted_iota(jnp.int32, gram.shape, 0)
    lane = lax.broadcasted_iota(jnp.int32, gram.shape, 1)
    return jnp.where(lane < SIDE, gram, jnp.where(lane - SIDE == row, 1.0, 0.0))


def eliminate(work, first, last):
    row = lax.broadcasted_iota(jnp.int32, work.shape, 0)
    for k in range(first, last):
        line = work[k : k + 1, :] / work[k : k + 1, k : k + 1]
        column = work[:, k : k + 1]
        work = jnp.where(row == k, line, work - column * line)
    return work


def end_inverse(work):
    zero = jnp.zeros_like(work)
    mask = low(work.shape)
    return jnp.concatenate([jnp.where(mask, swap(work), zero), jnp.where(mask, zero, work)], axis=0)


def inverse(gram):
    return end_inverse(eliminate(begin_inverse(gram), 0, SIDE))


def held(shape):
    return lax.broadcasted_iota(jnp.int32, shape, 0) % TILE >= LEAD


def pick(meta, at):
    lane = lax.broadcasted_iota(jnp.int32, meta.shape, 1)
    hit = (meta == (lane - at).astype(jnp.float32)) & (lane >= at) & (lane < at + OWNERS) & held(meta.shape)
    return jnp.where(hit, 1.0, 0.0)


def lines(ref):
    return ref[...].reshape(OWNERS * TILE, WIDE)


def prepare(given_ref, out_ref, place_ref):
    third = given_ref[:SIDE, :]
    twice = jnp.concatenate([third, third], axis=1)
    piece, gram = fold_halves(twice), fold_halves(product(third, twice, 0, 0))
    given = given_ref[SIDE:, :].astype(jnp.int32)
    place_ref[...] = given
    row = lax.broadcasted_iota(jnp.int32, given.shape, 0)
    lane = lax.broadcasted_iota(jnp.int32, given.shape, 1)
    first, second, third = (
        jnp.sum(jnp.where(lane == row - LEAD, given[n : n + 1, :], 0), axis=1, keepdims=True) for n in range(3)
    )
    row = lax.broadcasted_iota(jnp.int32, (TILE, WIDE), 0)
    lane = lax.broadcasted_iota(jnp.int32, (TILE, WIDE), 1)
    meta = jnp.where(
        lane < OWNERS,
        first % OWNERS,
        jnp.where(lane < 2 * OWNERS, second % OWNERS, third % PEERS * OWNERS + third // PEERS),
    )
    meta = jnp.where((row >= LEAD) & (row - LEAD < given[3:4, 0:1]), meta, -1)
    out_ref[...] = jnp.broadcast_to(meta.astype(jnp.float32)[None], out_ref.shape)
    out_ref[:, 0, :] = piece
    out_ref[:, 1, :] = gram


def arrange(second_ref, gram_ref, pairs_ref, turned):
    second = second_ref[...]
    gram_ref[...] = fold_halves(product(second, jnp.concatenate([second, second], axis=0), 1, 1))
    mask = low((HALF, WIDE))
    for pair in range(OWNERS // 2):
        tile = second[:, pair * WIDE : (pair + 1) * WIDE]
        turned[pair % 2] = jnp.concatenate([tile, tile], axis=0).T
        for n in range(2):
            even = turned[pair % 2, pl.ds(n * SIDE, HALF, stride=2), :]
            odd = turned[pair % 2, pl.ds(n * SIDE + 1, HALF, stride=2), :]
            pairs_ref[2 * pair + n] = jnp.where(mask, even, odd)


def relay(first_ref, gram_ref, out_ref):
    out_ref[:, :HALF, :] = jnp.broadcast_to(first_ref[:, 0, :][None], (PEERS, HALF, WIDE))
    second = gram_ref[pl.ds(lax.axis_index(SLAB), 1), :]
    third = jnp.sum(first_ref[:, 1, :], axis=0, keepdims=True)
    row = lax.broadcasted_iota(jnp.int32, (TILE, WIDE), 0)
    grams = jnp.where(row == 0, second, jnp.where(row == 1, third, 0.0))
    out_ref[:, HALF:, :] = jnp.broadcast_to(grams[None], (PEERS, TILE, WIDE))


def answer(meta_ref, held_ref, out_ref):
    wanted = lines(meta_ref)[:, 2 * OWNERS : 2 * OWNERS + 1]
    shape = (OWNERS * TILE, PEERS * OWNERS)
    lane = lax.broadcasted_iota(jnp.int32, shape, 1).astype(jnp.float32)
    stock = held_ref[:, :HALF, :].reshape(PEERS * OWNERS, WIDE)
    found = product(jnp.where((wanted == lane) & held(shape), 1.0, 0.0), stock)
    grams = jnp.sum(held_ref[:, HALF:, :], axis=0)
    out_ref[...] = found.reshape(OWNERS, TILE, WIDE)
    out_ref[:, 0, :] = jnp.broadcast_to(grams[0:1], (OWNERS, WIDE))
    out_ref[:, 1, :] = jnp.broadcast_to(grams[1:2], (OWNERS, WIDE))


def split(x):
    high = x.astype(jnp.bfloat16)
    return high, (x - high.astype(jnp.float32)).astype(jnp.bfloat16)


def fold(
    place_ref,
    blocks_ref,
    third_ref,
    pairs_ref,
    folded_ref,
    out_ref,
    inverse_ref,
    held,
    made,
    weights,
    held_sem,
    made_sem,
):
    def load(slot):
        return pltpu.make_async_copy(blocks_ref.at[slot], held.at[slot], held_sem.at[slot])

    def store(slot):
        return pltpu.make_async_copy(made.at[slot], folded_ref.at[slot], made_sem.at[slot])

    for slot in range(SLOTS):
        load(slot).start()
    for slot in range(SLOTS):
        packed = third_ref[:, slot + LEAD, :]
        mask, other = low(packed.shape), swap(packed)
        zero = jnp.zeros_like(packed)
        twin = jnp.concatenate(
            [
                jnp.where(mask, packed, zero),
                jnp.where(mask, other, zero),
                jnp.where(mask, zero, other),
                jnp.where(mask, zero, packed),
            ],
            axis=0,
        )
        high, rest = split(twin)
        twin = jnp.concatenate([high, rest], axis=1)
        weights[slot] = jnp.concatenate([twin, twin], axis=0)
    out_ref[:, :LEAD, :] = jnp.zeros((OWNERS, LEAD, WIDE), jnp.float32)
    work = begin_inverse(unfold_halves(third_ref[:, 0, :] * third_ref[:, 1, :]))
    work = eliminate(work, 0, BEFORE)
    groups, inner = SLOTS * HALF // STEP, SIDE - BEFORE - AFTER
    group = 0
    for slot in range(SLOTS):
        pairs = pairs_ref[place_ref[1, slot] % OWNERS]
        load(slot).wait()
        total = jnp.zeros((SIDE, WIDE), jnp.float32)
        for at in range(0, HALF, STEP):
            rows = jnp.concatenate(
                [held[slot, :, (at + n) * WIDE : (at + n + 1) * WIDE] for n in range(STEP)], axis=0
            )
            high, rest = split(rows)
            rows = jnp.concatenate([high, rest], axis=1)
            both = jnp.dot(rows, weights[slot], preferred_element_type=jnp.float32)
            both = both[:, :WIDE] + both[:, WIDE:]
            for n in range(STEP):
                piece = both[n * SIDE : (n + 1) * SIDE]
                made[slot, at + n] = piece
                total += piece * pairs[at + n : at + n + 1, :]
            work = eliminate(work, BEFORE + group * inner // groups, BEFORE + (group + 1) * inner // groups)
            group += 1
        store(slot).start()
        out_ref[:, slot + LEAD, :] = fold_halves(total + swap(total))
    inverse_ref[...] = end_inverse(eliminate(work, SIDE - AFTER, SIDE))
    for slot in range(SLOTS):
        store(slot).wait()


def solve_first(part_ref, meta_ref, inverse_ref, out_ref, solved_ref):
    chosen = pick(lines(meta_ref), 0)
    solved = product(product(chosen, lines(part_ref), 0, 0), inverse_ref[...])
    out_ref[...] = product(chosen, solved).reshape(OWNERS, TILE, WIDE)
    solved = solved[:OWNERS]
    out_ref[:, 0, :] = gram_packed(solved)
    solved_ref[...] = solved


def share_gram(first_ref, out_ref):
    total = jnp.sum(first_ref[:, 0, :], axis=0, keepdims=True)
    out_ref[...] = jnp.broadcast_to(total[None], out_ref.shape)


def contract(folded_ref, first_ref, out_ref, held, spaced, held_sem):
    def load(slot):
        return pltpu.make_async_copy(folded_ref.at[slot], held.at[slot], held_sem.at[slot])

    for slot in range(SLOTS):
        load(slot).start()
    out_ref[:, :LEAD, :] = jnp.zeros((OWNERS, LEAD, WIDE), jnp.float32)
    for slot in range(SLOTS):
        first = unfold_halves(first_ref[:, slot + LEAD, :])
        load(slot).wait()
        term = jnp.sum(held[slot] * first[None], axis=1)
        spaced[slot, pl.ds(0, HALF, stride=2), :] = term
        spaced[slot, pl.ds(1, HALF, stride=2), :] = swap(term)
        out_ref[:, slot + LEAD, :] = jnp.where(low(term.shape), spaced[slot, :HALF, :], swap(spaced[slot, HALF:, :]))


def insert(part_ref, square_ref, out_ref):
    out_ref[...] = part_ref[...]
    total = jnp.sum(square_ref[:, 0, :], axis=0, keepdims=True)
    out_ref[:, 0, :] = jnp.broadcast_to(total, (OWNERS, WIDE))


def sum_second(part_ref, meta_ref, solved_ref, out_ref):
    total = product(pick(lines(meta_ref), OWNERS), lines(part_ref), 0, 0)[OWNERS : 2 * OWNERS]
    both = jnp.concatenate([total, solved_ref[...]], axis=0)
    out_ref[...] = jnp.broadcast_to(both[None], out_ref.shape)


def invert_second(part_ref, third_ref, out_ref, scale_ref):
    square = unfold_halves(part_ref[:, 0, :])
    shape = square.shape
    row = lax.broadcasted_iota(jnp.int32, shape, 0)
    lane = lax.broadcasted_iota(jnp.int32, shape, 1)
    means = jnp.where(row == lane % SIDE, square, 0.0) / ROWS
    along = jnp.sqrt(jnp.sum(means, axis=0, keepdims=True) + 1e-06)
    down = jnp.sqrt(jnp.sum(jnp.where(lane < SIDE, means, 0.0), axis=1, keepdims=True) + 1e-06)
    scale_ref[...] = along
    out_ref[...] = inverse(square / along / down * unfold_halves(third_ref[:, 1, :]))


def solve_second(near_ref, inverse_ref, scale_ref, out_ref, square_ref):
    near = near_ref[...] / scale_ref[...]
    solved = product(near[:, :HALF].reshape(PEERS * HALF, WIDE), inverse_ref[...])
    out_ref[:, :HALF, :] = solved.reshape(PEERS, HALF, WIDE)
    out_ref[:, HALF:, :] = near[:, HALF:]
    total = jnp.sum(solved * solved, axis=0, keepdims=True)
    square_ref[...] = jnp.broadcast_to(total[None], square_ref.shape)


def turn(solved_ref, out_ref):
    mask = low((HALF, WIDE))
    half = OWNERS // 2
    for pair in range(half // 2):
        parts = []
        for block in (2 * pair, 2 * pair + 1):
            left, right = solved_ref[:, block, :], solved_ref[:, block + half, :]
            parts += [jnp.where(mask, left, swap(right)), jnp.where(mask, swap(left), right)]
        both = jnp.concatenate(parts, axis=0).T
        out_ref[:, pair * WIDE : (pair + 1) * WIDE] = both[:SIDE]
        out_ref[:, GROUP // 2 + pair * WIDE : GROUP // 2 + (pair + 1) * WIDE] = both[SIDE:]


def collect(which, own_ref, one_ref, two_ref, three_ref, out_ref, solved):
    own = lax.axis_index("x")
    for step, part in enumerate((own_ref, one_ref, two_ref, three_ref)):
        rows = part[:, which * HALF : (which + 1) * HALF, :]
        solved[pl.ds((own + TURNS - step) % TURNS * PEERS, PEERS)] = rows
    turn(solved, out_ref)


def collect_first(*refs):
    collect(1, *refs)


def collect_second(*refs):
    collect(0, *refs)


def finish(turned_ref, square_ref, new_ref, scale_ref):
    total = jnp.sum(square_ref[:, 0, :], axis=0, keepdims=True)
    scale = jnp.sqrt((total + swap(total)) / ROWS + 1e-06)
    scale_ref[...] = scale[:, :SIDE]
    shape = (SIDE, WIDE)
    row, lane = lax.broadcasted_iota(jnp.int32, shape, 0), lax.broadcasted_iota(jnp.int32, shape, 1)
    down = jnp.sum(jnp.where(row == lane, scale, 0.0), axis=1, keepdims=True)
    new_ref[...] = turned_ref[...] / down


def struct(*shape):
    return jax.ShapeDtypeStruct(shape, jnp.float32)


def exchange(x, axis):
    return lax.all_to_all(x, axis, 0, 0, tiled=True)


def call(body, *outs):
    return pl.pallas_call(body, out_shape=outs if len(outs) > 1 else outs[0], compiler_params=LIMIT)


def shards(blocks, coords, counts, factor_b, factor_c):
    scalars = pl.BlockSpec(memory_space=pltpu.SMEM)
    local = pl.BlockSpec(memory_space=pltpu.VMEM)
    apart = pl.BlockSpec(memory_space=pltpu.HBM)
    small = (OWNERS, TILE, WIDE)
    full = (OWNERS, HALF, WIDE)
    given = jnp.pad(coords, ((0, SIDE - SLOTS), (SIDE, TILE - 3))).T.astype(jnp.float32)
    row = lax.broadcasted_iota(jnp.int32, given.shape, 0)
    given = jnp.where(row < SIDE, jnp.pad(factor_c, ((0, TILE), (0, 0))), given)
    given = jnp.where(row < SIDE + 3, given, counts.astype(jnp.float32)[:, None])
    opening, place = pl.pallas_call(
        prepare,
        out_shape=(struct(*small), jax.ShapeDtypeStruct((TILE, SIDE), jnp.int32)),
        compiler_params=LIMIT,
    )(given)
    meta = exchange(opening, SLAB)
    gram_b, pairs = pl.pallas_call(
        arrange,
        out_shape=(struct(HALF, WIDE), struct(*full)),
        scratch_shapes=[pltpu.VMEM((2, WIDE, WIDE), jnp.float32)],
        compiler_params=LIMIT,
    )(factor_b.T)
    held = exchange(call(relay, struct(PEERS, HALF + TILE, WIDE))(meta, gram_b), "rows")
    third = exchange(call(answer, struct(*small))(meta, held), SLAB)
    folded, part_a, inverse_a = pl.pallas_call(
        fold,
        in_specs=[scalars, apart, local, local],
        out_specs=[apart, local, local],
        out_shape=(struct(SLOTS, HALF, SIDE, WIDE), struct(*small), struct(WIDE, WIDE)),
        scratch_shapes=[
            pltpu.VMEM((SLOTS, SIDE, SIDE * SIDE), jnp.float32),
            pltpu.VMEM((SLOTS, HALF, SIDE, WIDE), jnp.float32),
            pltpu.VMEM((SLOTS, 2 * WIDE, 2 * WIDE), jnp.bfloat16),
            pltpu.SemaphoreType.DMA((SLOTS,)),
            pltpu.SemaphoreType.DMA((SLOTS,)),
        ],
        compiler_params=LARGE,
    )(place, blocks, third, pairs)
    part_a = exchange(part_a, SLAB)
    answer_a, solved_a = call(solve_first, struct(*small), struct(HALF, WIDE))(part_a, meta, inverse_a)
    first = exchange(answer_a, SLAB)
    square_a = exchange(call(share_gram, struct(PEERS, TILE, WIDE))(first), "rows")
    part_b = pl.pallas_call(
        contract,
        in_specs=[apart, local],
        out_specs=local,
        out_shape=struct(*small),
        scratch_shapes=[
            pltpu.VMEM((SLOTS, HALF, SIDE, WIDE), jnp.float32),
            pltpu.VMEM((SLOTS, SIDE, WIDE), jnp.float32),
            pltpu.SemaphoreType.DMA((SLOTS,)),
        ],
        compiler_params=LARGE,
    )(folded, first)
    part_b = exchange(call(insert, struct(*small))(part_b, square_a), SLAB)
    near = exchange(call(sum_second, struct(PEERS, SIDE, WIDE))(part_b, meta, solved_a), "z")
    inverse_b, scale_a = call(invert_second, struct(WIDE, WIDE), struct(1, WIDE))(part_b, third)
    near, square_b = call(solve_second, struct(PEERS, SIDE, WIDE), struct(*small))(near, inverse_b, scale_a)
    parts = [near] + [
        lax.ppermute(near, "x", [(n, (n + step) % TURNS) for n in range(TURNS)]) for step in range(1, TURNS)
    ]
    square_b = exchange(square_b, ("x", "rows"))
    scratch = [pltpu.VMEM(full, jnp.float32)]
    new_a, turned_b = (
        pl.pallas_call(body, out_shape=struct(SIDE, GROUP), scratch_shapes=scratch, compiler_params=LIMIT)(*parts)
        for body in (collect_first, collect_second)
    )
    new_b, scale_b = call(finish, struct(SIDE, GROUP), struct(1, SIDE))(turned_b, square_b)
    return (new_a.T, new_b.T, scale_b.reshape(SIDE))


def solution(mesh):
    mesh = Mesh(mesh.devices.reshape(TURNS, PEERS, PEERS), ("x", "z", "rows"))
    split = ("x", "z", "rows")
    in_specs = (P(split, None, None), P(split, None), P(split), P("rows", None), P(split, None))
    out_specs = (P("rows", None), P("rows", None), P())
    return jax.shard_map(shards, mesh=mesh, in_specs=in_specs, out_specs=out_specs, check_vma=False)
```

```python
import jax
import jax.numpy as jnp
from jax import lax
from jax.experimental import pallas as pl
from jax.experimental.pallas import tpu as pltpu
from jax.sharding import Mesh
from jax.sharding import PartitionSpec as P

SIDE = 64
HALF = 32
WIDE = 128
STEP = 8
BEFORE = 10
AFTER = 8
TILE = 8
SLOTS = 6
LEAD = 2
TURNS = 4
PEERS = 8
OWNERS = 32
GROUP = 2048
ROWS = 16384
HIGH = lax.Precision.HIGHEST
SLAB = ("x", "z")
LIMIT = pltpu.CompilerParams(vmem_limit_bytes=24 * 1024 * 1024)
LARGE = pltpu.CompilerParams(vmem_limit_bytes=48 * 1024 * 1024)


def low(shape):
    return lax.broadcasted_iota(jnp.int32, shape, len(shape) - 1) < SIDE


def swap(x):
    return pltpu.roll(x, SIDE, 1)


def unfold_halves(packed):
    mask, other = low(packed.shape), swap(packed)
    return jnp.concatenate([jnp.where(mask, packed, other), jnp.where(mask, other, packed)], axis=0)


def fold_halves(rows):
    return jnp.where(low((HALF, WIDE)), rows[:HALF], rows[HALF:])


def product(left, right, left_dim=1, right_dim=0):
    return lax.dot_general(
        left,
        right,
        (((left_dim,), (right_dim,)), ((), ())),
        precision=HIGH,
        preferred_element_type=jnp.float32,
    )


def gram_packed(packed):
    both = product(packed, packed, 0, 0)
    total = both[:SIDE] + swap(both[SIDE:])
    return fold_halves(jnp.where(low(total.shape), total, swap(total)))


def begin_inverse(gram):
    row = lax.broadcasted_iota(jnp.int32, gram.shape, 0)
    lane = lax.broadcasted_iota(jnp.int32, gram.shape, 1)
    return jnp.where(lane < SIDE, gram, jnp.where(lane - SIDE == row, 1.0, 0.0))


def eliminate(work, first, last):
    row = lax.broadcasted_iota(jnp.int32, work.shape, 0)
    for k in range(first, last):
        line = work[k : k + 1, :] / work[k : k + 1, k : k + 1]
        column = work[:, k : k + 1]
        work = jnp.where(row == k, line, work - column * line)
    return work


def end_inverse(work):
    zero = jnp.zeros_like(work)
    mask = low(work.shape)
    return jnp.concatenate([jnp.where(mask, swap(work), zero), jnp.where(mask, zero, work)], axis=0)


def inverse(gram):
    return end_inverse(eliminate(begin_inverse(gram), 0, SIDE))


def held(shape):
    return lax.broadcasted_iota(jnp.int32, shape, 0) % TILE >= LEAD


def pick(meta):
    lane = lax.broadcasted_iota(jnp.int32, meta.shape, 1)
    hit = (meta == (lane % OWNERS).astype(jnp.float32)) & (lane < 2 * OWNERS) & held(meta.shape)
    return jnp.where(hit, 1.0, 0.0)


def choose(chosen, values, chosen_dim=0):
    high = values.astype(jnp.bfloat16)
    rest = values - high.astype(jnp.float32)
    middle = rest.astype(jnp.bfloat16)
    last = (rest - middle.astype(jnp.float32)).astype(jnp.bfloat16)
    parts = lax.dot_general(
        chosen,
        jnp.concatenate([high, middle, last], axis=1),
        (((1 - chosen_dim,), (0,)), ((), ())),
        preferred_element_type=jnp.float32,
    )
    return parts[:, :WIDE] + (parts[:, WIDE : 2 * WIDE] + parts[:, 2 * WIDE :])


def lines(ref):
    return ref[...].reshape(OWNERS * TILE, WIDE)


def prepare(given_ref, out_ref, place_ref):
    third = given_ref[:SIDE, :]
    twice = jnp.concatenate([third, third], axis=1)
    piece, gram = fold_halves(twice), fold_halves(product(third, twice, 0, 0))
    given = given_ref[SIDE:, :].astype(jnp.int32)
    place_ref[...] = given
    row = lax.broadcasted_iota(jnp.int32, given.shape, 0)
    lane = lax.broadcasted_iota(jnp.int32, given.shape, 1)
    first, second, third = (
        jnp.sum(jnp.where(lane == row - LEAD, given[n : n + 1, :], 0), axis=1, keepdims=True) for n in range(3)
    )
    row = lax.broadcasted_iota(jnp.int32, (TILE, WIDE), 0)
    lane = lax.broadcasted_iota(jnp.int32, (TILE, WIDE), 1)
    meta = jnp.where(
        lane < OWNERS,
        first % OWNERS,
        jnp.where(lane < 2 * OWNERS, second % OWNERS, third % PEERS * OWNERS + third // PEERS),
    )
    meta = jnp.where((row >= LEAD) & (row - LEAD < given[3:4, 0:1]), meta, -1)
    out_ref[...] = jnp.broadcast_to(meta.astype(jnp.float32)[None], out_ref.shape)
    out_ref[:, 0, :] = piece
    out_ref[:, 1, :] = gram


def arrange(second_ref, gram_ref, pairs_ref, turned):
    second = second_ref[...]
    gram_ref[...] = fold_halves(product(second, jnp.concatenate([second, second], axis=0), 1, 1))
    mask = low((HALF, WIDE))
    for pair in range(OWNERS // 2):
        tile = second[:, pair * WIDE : (pair + 1) * WIDE]
        turned[pair % 2] = jnp.concatenate([tile, tile], axis=0).T
        for n in range(2):
            even = turned[pair % 2, pl.ds(n * SIDE, HALF, stride=2), :]
            odd = turned[pair % 2, pl.ds(n * SIDE + 1, HALF, stride=2), :]
            pairs_ref[2 * pair + n] = jnp.where(mask, even, odd)


def relay(first_ref, gram_ref, out_ref):
    out_ref[:, :HALF, :] = jnp.broadcast_to(first_ref[:, 0, :][None], (PEERS, HALF, WIDE))
    second = gram_ref[pl.ds(lax.axis_index(SLAB), 1), :]
    third = jnp.sum(first_ref[:, 1, :], axis=0, keepdims=True)
    row = lax.broadcasted_iota(jnp.int32, (TILE, WIDE), 0)
    grams = jnp.where(row == 0, second, jnp.where(row == 1, third, 0.0))
    out_ref[:, HALF:, :] = jnp.broadcast_to(grams[None], (PEERS, TILE, WIDE))


def answer(meta_ref, held_ref, out_ref):
    wanted = lines(meta_ref)[:, 2 * OWNERS : 2 * OWNERS + 1]
    shape = (OWNERS * TILE, PEERS * OWNERS)
    lane = lax.broadcasted_iota(jnp.int32, shape, 1).astype(jnp.float32)
    stock = held_ref[:, :HALF, :].reshape(PEERS * OWNERS, WIDE)
    found = choose(jnp.where((wanted == lane) & held(shape), 1.0, 0.0).astype(jnp.bfloat16), stock)
    grams = jnp.sum(held_ref[:, HALF:, :], axis=0)
    out_ref[...] = found.reshape(OWNERS, TILE, WIDE)
    out_ref[:, 0, :] = jnp.broadcast_to(grams[0:1], (OWNERS, WIDE))
    out_ref[:, 1, :] = jnp.broadcast_to(grams[1:2], (OWNERS, WIDE))


def split(x):
    high = x.astype(jnp.bfloat16)
    return high, (x - high.astype(jnp.float32)).astype(jnp.bfloat16)


def fold(
    place_ref,
    blocks_ref,
    third_ref,
    pairs_ref,
    folded_ref,
    out_ref,
    inverse_ref,
    held,
    made,
    weights,
    held_sem,
    made_sem,
):
    def load(slot):
        return pltpu.make_async_copy(blocks_ref.at[slot], held.at[slot], held_sem.at[slot])

    def store(slot):
        return pltpu.make_async_copy(made.at[slot], folded_ref.at[slot], made_sem.at[slot])

    for slot in range(SLOTS):
        load(slot).start()
    for slot in range(SLOTS):
        packed = third_ref[:, slot + LEAD, :]
        mask, other = low(packed.shape), swap(packed)
        zero = jnp.zeros_like(packed)
        twin = jnp.concatenate(
            [
                jnp.where(mask, packed, zero),
                jnp.where(mask, other, zero),
                jnp.where(mask, zero, other),
                jnp.where(mask, zero, packed),
            ],
            axis=0,
        )
        high, rest = split(twin)
        twin = jnp.concatenate([high, rest], axis=1)
        weights[slot] = jnp.concatenate([twin, twin], axis=0)
    out_ref[:, :LEAD, :] = jnp.zeros((OWNERS, LEAD, WIDE), jnp.float32)
    work = begin_inverse(unfold_halves(third_ref[:, 0, :] * third_ref[:, 1, :]))
    work = eliminate(work, 0, BEFORE)
    groups, inner = SLOTS * HALF // STEP, SIDE - BEFORE - AFTER
    group = 0
    for slot in range(SLOTS):
        pairs = pairs_ref[place_ref[1, slot] % OWNERS]
        load(slot).wait()
        total = jnp.zeros((SIDE, WIDE), jnp.float32)
        for at in range(0, HALF, STEP):
            rows = jnp.concatenate(
                [held[slot, :, (at + n) * WIDE : (at + n + 1) * WIDE] for n in range(STEP)], axis=0
            )
            high, rest = split(rows)
            rows = jnp.concatenate([high, rest], axis=1)
            both = jnp.dot(rows, weights[slot], preferred_element_type=jnp.float32)
            both = both[:, :WIDE] + both[:, WIDE:]
            for n in range(STEP):
                piece = both[n * SIDE : (n + 1) * SIDE]
                made[slot, at + n] = piece
                total += piece * pairs[at + n : at + n + 1, :]
            work = eliminate(work, BEFORE + group * inner // groups, BEFORE + (group + 1) * inner // groups)
            group += 1
        store(slot).start()
        out_ref[:, slot + LEAD, :] = fold_halves(total + swap(total))
    inverse_ref[...] = end_inverse(eliminate(work, SIDE - AFTER, SIDE))
    for slot in range(SLOTS):
        store(slot).wait()


def solve_first(part_ref, meta_ref, inverse_ref, out_ref, solved_ref):
    chosen = pick(lines(meta_ref)).astype(jnp.bfloat16)
    solved = product(choose(chosen, lines(part_ref), 1)[:OWNERS], inverse_ref[...])
    solved_ref[...] = solved
    blank = jnp.zeros((WIDE - OWNERS, WIDE), jnp.float32)
    out_ref[...] = choose(chosen, jnp.concatenate([solved, blank], axis=0)).reshape(OWNERS, TILE, WIDE)
    out_ref[:, 0, :] = gram_packed(solved)


def share_gram(first_ref, out_ref):
    total = jnp.sum(first_ref[:, 0, :], axis=0, keepdims=True)
    out_ref[...] = jnp.broadcast_to(total, out_ref.shape)


def contract(folded_ref, first_ref, meta_ref, out_ref, turned_ref, held, spaced, held_sem):
    def load(slot):
        return pltpu.make_async_copy(folded_ref.at[slot], held.at[slot], held_sem.at[slot])

    for slot in range(SLOTS):
        load(slot).start()
    out_ref[:, :LEAD, :] = jnp.zeros((OWNERS, LEAD, WIDE), jnp.float32)
    turned_ref[...] = pick(lines(meta_ref)).T.astype(jnp.bfloat16)
    for slot in range(SLOTS):
        first = unfold_halves(first_ref[:, slot + LEAD, :])
        load(slot).wait()
        term = jnp.sum(held[slot] * first[None], axis=1)
        spaced[slot, pl.ds(0, HALF, stride=2), :] = term
        spaced[slot, pl.ds(1, HALF, stride=2), :] = swap(term)
        out_ref[:, slot + LEAD, :] = jnp.where(low(term.shape), spaced[slot, :HALF, :], swap(spaced[slot, HALF:, :]))


def insert(part_ref, square_ref, other_ref, out_ref):
    out_ref[...] = part_ref[...]
    out_ref[:, 0, :] = jnp.broadcast_to(square_ref[0:1, :] + other_ref[0:1, :], (OWNERS, WIDE))


def sum_second(part_ref, turned_ref, solved_ref, out_ref, square_ref):
    total = choose(turned_ref[OWNERS : 2 * OWNERS, :], lines(part_ref))
    both = jnp.concatenate([total, solved_ref[...]], axis=0)
    out_ref[...] = jnp.broadcast_to(both[None], out_ref.shape)
    square_ref[...] = part_ref[:, 0, :]


def invert_second(own_ref, one_ref, two_ref, three_ref, third_ref, out_ref, scale_ref):
    square = unfold_halves(own_ref[...] + one_ref[...] + two_ref[...] + three_ref[...])
    shape = square.shape
    row = lax.broadcasted_iota(jnp.int32, shape, 0)
    lane = lax.broadcasted_iota(jnp.int32, shape, 1)
    means = jnp.where(row == lane % SIDE, square, 0.0) / ROWS
    along = jnp.sqrt(jnp.sum(means, axis=0, keepdims=True) + 1e-06)
    down = jnp.sqrt(jnp.sum(jnp.where(lane < SIDE, means, 0.0), axis=1, keepdims=True) + 1e-06)
    scale_ref[...] = 1.0 / along
    out_ref[...] = inverse(square / along / down * unfold_halves(third_ref[:, 1, :]))


def solve_second(near_ref, inverse_ref, scale_ref, out_ref, square_ref):
    near = near_ref[...] * scale_ref[...]
    solved = product(near[:, :HALF].reshape(PEERS * HALF, WIDE), inverse_ref[...])
    out_ref[:, :HALF, :] = solved.reshape(PEERS, HALF, WIDE)
    out_ref[:, HALF:, :] = near[:, HALF:]
    total = jnp.sum(solved * solved, axis=0, keepdims=True)
    square_ref[...] = jnp.broadcast_to(total[None], square_ref.shape)


def turn(solved_ref, out_ref):
    mask = low((HALF, WIDE))
    half = OWNERS // 2
    for pair in range(half // 2):
        parts = []
        for block in (2 * pair, 2 * pair + 1):
            left, right = solved_ref[:, block, :], solved_ref[:, block + half, :]
            parts += [jnp.where(mask, left, swap(right)), jnp.where(mask, swap(left), right)]
        both = jnp.concatenate(parts, axis=0).T
        out_ref[:, pair * WIDE : (pair + 1) * WIDE] = both[:SIDE]
        out_ref[:, GROUP // 2 + pair * WIDE : GROUP // 2 + (pair + 1) * WIDE] = both[SIDE:]


def collect(which, own_ref, one_ref, two_ref, three_ref, out_ref, solved):
    own = lax.axis_index("x")
    for step, part in enumerate((own_ref, one_ref, two_ref, three_ref)):
        rows = part[:, which * HALF : (which + 1) * HALF, :]
        solved[pl.ds((own + TURNS - step) % TURNS * PEERS, PEERS)] = rows
    turn(solved, out_ref)


def collect_first(*refs):
    collect(1, *refs)


def collect_second(*refs):
    collect(0, *refs)


def finish(turned_ref, square_ref, new_ref, scale_ref):
    total = jnp.sum(square_ref[:, 0, :], axis=0, keepdims=True)
    scale = jnp.sqrt((total + swap(total)) / ROWS + 1e-06)
    scale_ref[...] = scale[:, :SIDE]
    shape = (SIDE, WIDE)
    row, lane = lax.broadcasted_iota(jnp.int32, shape, 0), lax.broadcasted_iota(jnp.int32, shape, 1)
    down = jnp.sum(jnp.where(row == lane, scale, 0.0), axis=1, keepdims=True)
    new_ref[...] = turned_ref[...] * (1.0 / down)


def struct(*shape):
    return jax.ShapeDtypeStruct(shape, jnp.float32)


def exchange(x, axis):
    return lax.all_to_all(x, axis, 0, 0, tiled=True)


def call(body, *outs):
    return pl.pallas_call(body, out_shape=outs if len(outs) > 1 else outs[0], compiler_params=LIMIT)


def shards(blocks, coords, counts, factor_b, factor_c):
    scalars = pl.BlockSpec(memory_space=pltpu.SMEM)
    local = pl.BlockSpec(memory_space=pltpu.VMEM)
    apart = pl.BlockSpec(memory_space=pltpu.HBM)
    small = (OWNERS, TILE, WIDE)
    full = (OWNERS, HALF, WIDE)
    given = jnp.pad(coords, ((0, SIDE - SLOTS), (SIDE, TILE - 3))).T.astype(jnp.float32)
    row = lax.broadcasted_iota(jnp.int32, given.shape, 0)
    given = jnp.where(row < SIDE, jnp.pad(factor_c, ((0, TILE), (0, 0))), given)
    given = jnp.where(row < SIDE + 3, given, counts.astype(jnp.float32)[:, None])
    opening, place = pl.pallas_call(
        prepare,
        out_shape=(struct(*small), jax.ShapeDtypeStruct((TILE, SIDE), jnp.int32)),
        compiler_params=LIMIT,
    )(given)
    meta = exchange(opening, SLAB)
    gram_b, pairs = pl.pallas_call(
        arrange,
        out_shape=(struct(HALF, WIDE), struct(*full)),
        scratch_shapes=[pltpu.VMEM((2, WIDE, WIDE), jnp.float32)],
        compiler_params=LIMIT,
    )(factor_b.T)
    held = exchange(call(relay, struct(PEERS, HALF + TILE, WIDE))(meta, gram_b), "rows")
    third = exchange(call(answer, struct(*small))(meta, held), SLAB)
    folded, part_a, inverse_a = pl.pallas_call(
        fold,
        in_specs=[scalars, apart, local, local],
        out_specs=[apart, local, local],
        out_shape=(struct(SLOTS, HALF, SIDE, WIDE), struct(*small), struct(WIDE, WIDE)),
        scratch_shapes=[
            pltpu.VMEM((SLOTS, SIDE, SIDE * SIDE), jnp.float32),
            pltpu.VMEM((SLOTS, HALF, SIDE, WIDE), jnp.float32),
            pltpu.VMEM((SLOTS, 2 * WIDE, 2 * WIDE), jnp.bfloat16),
            pltpu.SemaphoreType.DMA((SLOTS,)),
            pltpu.SemaphoreType.DMA((SLOTS,)),
        ],
        compiler_params=LARGE,
    )(place, blocks, third, pairs)
    part_a = exchange(part_a, SLAB)
    answer_a, solved_a = call(solve_first, struct(*small), struct(HALF, WIDE))(part_a, meta, inverse_a)
    first = exchange(answer_a, SLAB)
    first, square_a = lax.optimization_barrier((first, call(share_gram, struct(TILE, WIDE))(first)))
    other_a = lax.ppermute(square_a, "rows", [(n, n ^ 1) for n in range(PEERS)])
    part_b, turned = pl.pallas_call(
        contract,
        in_specs=[apart, local, local],
        out_specs=[local, local],
        out_shape=(struct(*small), jax.ShapeDtypeStruct((WIDE, OWNERS * TILE), jnp.bfloat16)),
        scratch_shapes=[
            pltpu.VMEM((SLOTS, HALF, SIDE, WIDE), jnp.float32),
            pltpu.VMEM((SLOTS, SIDE, WIDE), jnp.float32),
            pltpu.SemaphoreType.DMA((SLOTS,)),
        ],
        compiler_params=LARGE,
    )(folded, first, meta)
    part_b = exchange(call(insert, struct(*small))(part_b, square_a, other_a), SLAB)
    near, square_a = call(sum_second, struct(PEERS, SIDE, WIDE), struct(HALF, WIDE))(part_b, turned, solved_a)
    squares_a = [square_a] + [
        lax.ppermute(square_a, "rows", [(n, (n + 2 * step) % PEERS) for n in range(PEERS)])
        for step in range(1, TURNS)
    ]
    near = exchange(near, "z")
    inverse_b, scale_a = call(invert_second, struct(WIDE, WIDE), struct(1, WIDE))(*squares_a, third)
    near, square_b = call(solve_second, struct(PEERS, SIDE, WIDE), struct(*small))(near, inverse_b, scale_a)
    parts = [near] + [
        lax.ppermute(near, "x", [(n, (n + step) % TURNS) for n in range(TURNS)]) for step in range(1, TURNS)
    ]
    square_b = exchange(square_b, ("x", "rows"))
    scratch = [pltpu.VMEM(full, jnp.float32)]
    new_a, turned_b = (
        pl.pallas_call(body, out_shape=struct(SIDE, GROUP), scratch_shapes=scratch, compiler_params=LIMIT)(*parts)
        for body in (collect_first, collect_second)
    )
    new_b, scale_b = call(finish, struct(SIDE, GROUP), struct(1, SIDE))(turned_b, square_b)
    return (new_a.T, new_b.T, scale_b.reshape(SIDE))


def solution(mesh):
    mesh = Mesh(mesh.devices.reshape(TURNS, PEERS, PEERS), ("x", "z", "rows"))
    split = ("x", "z", "rows")
    in_specs = (P(split, None, None), P(split, None), P(split), P("rows", None), P(split, None))
    out_specs = (P("rows", None), P("rows", None), P())
    return jax.shard_map(shards, mesh=mesh, in_specs=in_specs, out_specs=out_specs, check_vma=False)
```

```python
import jax
import jax.numpy as jnp
from jax import lax
from jax.experimental import pallas as pl
from jax.experimental.pallas import tpu as pltpu
from jax.sharding import Mesh
from jax.sharding import PartitionSpec as P

SIDE = 64
HALF = 32
WIDE = 128
STEP = 8
BEFORE = 14
AFTER = 12
TILE = 8
SLOTS = 6
LEAD = 2
TURNS = 4
PEERS = 8
OWNERS = 32
GROUP = 2048
ROWS = 16384
HIGH = lax.Precision.HIGHEST
SLAB = ("x", "z")
LIMIT = pltpu.CompilerParams(vmem_limit_bytes=24 * 1024 * 1024)
LARGE = pltpu.CompilerParams(vmem_limit_bytes=48 * 1024 * 1024)


def low(shape):
    return lax.broadcasted_iota(jnp.int32, shape, len(shape) - 1) < SIDE


def swap(x):
    return pltpu.roll(x, SIDE, 1)


def unfold_halves(packed):
    mask, other = low(packed.shape), swap(packed)
    return jnp.concatenate([jnp.where(mask, packed, other), jnp.where(mask, other, packed)], axis=0)


def fold_halves(rows):
    return jnp.where(low((HALF, WIDE)), rows[:HALF], rows[HALF:])


def product(left, right, left_dim=1, right_dim=0):
    return lax.dot_general(
        left,
        right,
        (((left_dim,), (right_dim,)), ((), ())),
        precision=HIGH,
        preferred_element_type=jnp.float32,
    )


def gram_packed(packed):
    both = product(packed, packed, 0, 0)
    total = both[:SIDE] + swap(both[SIDE:])
    return fold_halves(jnp.where(low(total.shape), total, swap(total)))


def spot(work, row, lane):
    return jnp.broadcast_to(work[row : row + 1, lane : lane + 1], (TILE, WIDE))


def begin_inverse(gram):
    row = lax.broadcasted_iota(jnp.int32, gram.shape, 0)
    lane = lax.broadcasted_iota(jnp.int32, gram.shape, 1)
    return jnp.where(lane < SIDE, gram, jnp.where(lane - SIDE == row, 1.0, 0.0))


def eliminate(work, first, last):
    row = lax.broadcasted_iota(jnp.int32, work.shape, 0)
    for k in range(first, last):
        line = work[k : k + 1, :] / work[k : k + 1, k : k + 1]
        column = work[:, k : k + 1]
        work = jnp.where(row == k, line, work - column * line)
    return work


def eliminate_all(work):
    row = lax.broadcasted_iota(jnp.int32, work.shape, 0)
    ratio = 1.0 / spot(work, 0, 0)
    for k in range(SIDE):
        line = jnp.broadcast_to(work[k : k + 1, :], (TILE, WIDE)) * ratio
        if k + 1 < SIDE:
            ratio = 1.0 / (spot(work, k + 1, k + 1) - spot(work, k + 1, k) * (spot(work, k, k + 1) * ratio))
        line = jnp.broadcast_to(line[None], (TILE, TILE, WIDE)).reshape(work.shape)
        work = jnp.where(row == k, line, work - work[:, k : k + 1] * line)
    return work


def end_inverse(work):
    zero = jnp.zeros_like(work)
    mask = low(work.shape)
    return jnp.concatenate([jnp.where(mask, swap(work), zero), jnp.where(mask, zero, work)], axis=0)


def inverse(gram):
    return end_inverse(eliminate_all(begin_inverse(gram)))


def held(shape):
    return lax.broadcasted_iota(jnp.int32, shape, 0) % TILE >= LEAD


def pick(meta):
    lane = lax.broadcasted_iota(jnp.int32, meta.shape, 1)
    hit = (meta == (lane % OWNERS).astype(jnp.float32)) & (lane < 2 * OWNERS) & held(meta.shape)
    return jnp.where(hit, 1.0, 0.0)


def choose(chosen, values, chosen_dim=0):
    high = values.astype(jnp.bfloat16)
    rest = values - high.astype(jnp.float32)
    middle = rest.astype(jnp.bfloat16)
    last = (rest - middle.astype(jnp.float32)).astype(jnp.bfloat16)
    parts = lax.dot_general(
        chosen,
        jnp.concatenate([high, middle, last], axis=1),
        (((1 - chosen_dim,), (0,)), ((), ())),
        preferred_element_type=jnp.float32,
    )
    return parts[:, :WIDE] + (parts[:, WIDE : 2 * WIDE] + parts[:, 2 * WIDE :])


def lines(ref):
    return ref[...].reshape(OWNERS * TILE, WIDE)


def prepare(given_ref, out_ref, place_ref):
    third = given_ref[:SIDE, :]
    twice = jnp.concatenate([third, third], axis=1)
    piece, gram = fold_halves(twice), fold_halves(product(third, twice, 0, 0))
    given = given_ref[SIDE:, :].astype(jnp.int32)
    place_ref[...] = given
    row = lax.broadcasted_iota(jnp.int32, given.shape, 0)
    lane = lax.broadcasted_iota(jnp.int32, given.shape, 1)
    first, second, third = (
        jnp.sum(jnp.where(lane == row - LEAD, given[n : n + 1, :], 0), axis=1, keepdims=True) for n in range(3)
    )
    row = lax.broadcasted_iota(jnp.int32, (TILE, WIDE), 0)
    lane = lax.broadcasted_iota(jnp.int32, (TILE, WIDE), 1)
    meta = jnp.where(
        lane < OWNERS,
        first % OWNERS,
        jnp.where(lane < 2 * OWNERS, second % OWNERS, third % PEERS * OWNERS + third // PEERS),
    )
    meta = jnp.where((row >= LEAD) & (row - LEAD < given[3:4, 0:1]), meta, -1)
    out_ref[...] = jnp.broadcast_to(meta.astype(jnp.float32)[None], out_ref.shape)
    out_ref[:, 0, :] = piece
    out_ref[:, 1, :] = gram


def arrange(second_ref, gram_ref, pairs_ref, turned):
    second = second_ref[...]
    gram_ref[...] = fold_halves(product(second, jnp.concatenate([second, second], axis=0), 1, 1))
    mask = low((HALF, WIDE))
    for pair in range(OWNERS // 2):
        tile = second[:, pair * WIDE : (pair + 1) * WIDE]
        turned[pair % 2] = jnp.concatenate([tile, tile], axis=0).T
        for n in range(2):
            even = turned[pair % 2, pl.ds(n * SIDE, HALF, stride=2), :]
            odd = turned[pair % 2, pl.ds(n * SIDE + 1, HALF, stride=2), :]
            pairs_ref[2 * pair + n] = jnp.where(mask, even, odd)


def relay(first_ref, gram_ref, out_ref):
    out_ref[:, :HALF, :] = jnp.broadcast_to(first_ref[:, 0, :][None], (PEERS, HALF, WIDE))
    second = gram_ref[pl.ds(lax.axis_index(SLAB), 1), :]
    third = jnp.sum(first_ref[:, 1, :], axis=0, keepdims=True)
    row = lax.broadcasted_iota(jnp.int32, (TILE, WIDE), 0)
    grams = jnp.where(row == 0, second, jnp.where(row == 1, third, 0.0))
    out_ref[:, HALF:, :] = jnp.broadcast_to(grams[None], (PEERS, TILE, WIDE))


def answer(meta_ref, held_ref, out_ref):
    wanted = lines(meta_ref)[:, 2 * OWNERS : 2 * OWNERS + 1]
    shape = (OWNERS * TILE, PEERS * OWNERS)
    lane = lax.broadcasted_iota(jnp.int32, shape, 1).astype(jnp.float32)
    stock = held_ref[:, :HALF, :].reshape(PEERS * OWNERS, WIDE)
    found = choose(jnp.where((wanted == lane) & held(shape), 1.0, 0.0).astype(jnp.bfloat16), stock)
    grams = jnp.sum(held_ref[:, HALF:, :], axis=0)
    out_ref[...] = found.reshape(OWNERS, TILE, WIDE)
    out_ref[:, 0, :] = jnp.broadcast_to(grams[0:1], (OWNERS, WIDE))
    out_ref[:, 1, :] = jnp.broadcast_to(grams[1:2], (OWNERS, WIDE))


def split(x):
    high = x.astype(jnp.bfloat16)
    return high, (x - high.astype(jnp.float32)).astype(jnp.bfloat16)


def fold(
    place_ref,
    blocks_ref,
    third_ref,
    pairs_ref,
    folded_ref,
    out_ref,
    inverse_ref,
    held,
    made,
    weights,
    held_sem,
    made_sem,
):
    def load(slot):
        return pltpu.make_async_copy(blocks_ref.at[slot], held.at[slot], held_sem.at[slot])

    def store(slot):
        return pltpu.make_async_copy(made.at[slot], folded_ref.at[slot], made_sem.at[slot])

    for slot in range(SLOTS):
        load(slot).start()
    for slot in range(SLOTS):
        packed = third_ref[:, slot + LEAD, :]
        mask, other = low(packed.shape), swap(packed)
        zero = jnp.zeros_like(packed)
        twin = jnp.concatenate(
            [
                jnp.where(mask, packed, zero),
                jnp.where(mask, other, zero),
                jnp.where(mask, zero, other),
                jnp.where(mask, zero, packed),
            ],
            axis=0,
        )
        high, rest = split(twin)
        twin = jnp.concatenate([high, rest], axis=1)
        weights[slot] = jnp.concatenate([twin, twin], axis=0)
    out_ref[:, :LEAD, :] = jnp.zeros((OWNERS, LEAD, WIDE), jnp.float32)
    work = begin_inverse(unfold_halves(third_ref[:, 0, :] * third_ref[:, 1, :]))
    work = eliminate(work, 0, BEFORE)
    groups, inner = SLOTS * HALF // STEP, SIDE - BEFORE - AFTER
    group = 0
    for slot in range(SLOTS):
        pairs = pairs_ref[place_ref[1, slot] % OWNERS]
        load(slot).wait()
        total = jnp.zeros((SIDE, WIDE), jnp.float32)
        for at in range(0, HALF, STEP):
            rows = jnp.concatenate(
                [held[slot, :, (at + n) * WIDE : (at + n + 1) * WIDE] for n in range(STEP)], axis=0
            )
            high, rest = split(rows)
            rows = jnp.concatenate([high, rest], axis=1)
            both = jnp.dot(rows, weights[slot], preferred_element_type=jnp.float32)
            both = both[:, :WIDE] + both[:, WIDE:]
            for n in range(STEP):
                piece = both[n * SIDE : (n + 1) * SIDE]
                made[slot, at + n] = piece
                total += piece * pairs[at + n : at + n + 1, :]
            work = eliminate(work, BEFORE + group * inner // groups, BEFORE + (group + 1) * inner // groups)
            group += 1
        store(slot).start()
        out_ref[:, slot + LEAD, :] = fold_halves(total + swap(total))
    inverse_ref[...] = end_inverse(eliminate(work, SIDE - AFTER, SIDE))
    for slot in range(SLOTS):
        store(slot).wait()


def solve_first(part_ref, meta_ref, inverse_ref, out_ref, solved_ref):
    chosen = pick(lines(meta_ref)).astype(jnp.bfloat16)
    solved = product(choose(chosen, lines(part_ref), 1)[:OWNERS], inverse_ref[...])
    solved_ref[...] = solved
    blank = jnp.zeros((WIDE - OWNERS, WIDE), jnp.float32)
    out_ref[...] = choose(chosen, jnp.concatenate([solved, blank], axis=0)).reshape(OWNERS, TILE, WIDE)
    out_ref[:, 0, :] = gram_packed(solved)


def share_gram(first_ref, out_ref):
    total = jnp.sum(first_ref[:, 0, :], axis=0, keepdims=True)
    out_ref[...] = jnp.broadcast_to(total, out_ref.shape)


def contract(folded_ref, first_ref, meta_ref, out_ref, turned_ref, held, spaced, held_sem):
    def load(slot):
        return pltpu.make_async_copy(folded_ref.at[slot], held.at[slot], held_sem.at[slot])

    for slot in range(SLOTS):
        load(slot).start()
    out_ref[:, :LEAD, :] = jnp.zeros((OWNERS, LEAD, WIDE), jnp.float32)
    turned_ref[...] = pick(lines(meta_ref)).T.astype(jnp.bfloat16)
    for slot in range(SLOTS):
        first = unfold_halves(first_ref[:, slot + LEAD, :])
        load(slot).wait()
        term = jnp.sum(held[slot] * first[None], axis=1)
        spaced[slot, pl.ds(0, HALF, stride=2), :] = term
        spaced[slot, pl.ds(1, HALF, stride=2), :] = swap(term)
        out_ref[:, slot + LEAD, :] = jnp.where(low(term.shape), spaced[slot, :HALF, :], swap(spaced[slot, HALF:, :]))


def insert(part_ref, square_ref, other_ref, out_ref):
    out_ref[...] = part_ref[...]
    out_ref[:, 0, :] = jnp.broadcast_to(square_ref[0:1, :] + other_ref[0:1, :], (OWNERS, WIDE))


def sum_second(part_ref, turned_ref, solved_ref, out_ref, square_ref):
    total = choose(turned_ref[OWNERS : 2 * OWNERS, :], lines(part_ref))
    both = jnp.concatenate([total, solved_ref[...]], axis=0)
    out_ref[...] = jnp.broadcast_to(both[None], out_ref.shape)
    square_ref[...] = part_ref[:, 0, :]


def invert_second(own_ref, one_ref, two_ref, three_ref, third_ref, out_ref, scale_ref):
    square = unfold_halves(own_ref[...] + one_ref[...] + two_ref[...] + three_ref[...])
    shape = square.shape
    row = lax.broadcasted_iota(jnp.int32, shape, 0)
    lane = lax.broadcasted_iota(jnp.int32, shape, 1)
    means = jnp.where(row == lane % SIDE, square, 0.0) / ROWS
    along = jnp.sqrt(jnp.sum(means, axis=0, keepdims=True) + 1e-06)
    down = jnp.sqrt(jnp.sum(jnp.where(lane < SIDE, means, 0.0), axis=1, keepdims=True) + 1e-06)
    scale_ref[...] = 1.0 / along
    out_ref[...] = inverse(square / along / down * unfold_halves(third_ref[:, 1, :]))


def solve_second(near_ref, inverse_ref, scale_ref, out_ref, square_ref):
    near = near_ref[...] * scale_ref[...]
    solved = product(near[:, :HALF].reshape(PEERS * HALF, WIDE), inverse_ref[...])
    out_ref[:, :HALF, :] = solved.reshape(PEERS, HALF, WIDE)
    out_ref[:, HALF:, :] = near[:, HALF:]
    total = jnp.sum(solved * solved, axis=0, keepdims=True)
    square_ref[...] = jnp.broadcast_to(total[None], square_ref.shape)


def turn(solved_ref, out_ref):
    mask = low((HALF, WIDE))
    half = OWNERS // 2
    for pair in range(half // 2):
        parts = []
        for block in (2 * pair, 2 * pair + 1):
            left, right = solved_ref[:, block, :], solved_ref[:, block + half, :]
            parts += [jnp.where(mask, left, swap(right)), jnp.where(mask, swap(left), right)]
        both = jnp.concatenate(parts, axis=0).T
        out_ref[:, pair * WIDE : (pair + 1) * WIDE] = both[:SIDE]
        out_ref[:, GROUP // 2 + pair * WIDE : GROUP // 2 + (pair + 1) * WIDE] = both[SIDE:]


def collect(which, own_ref, one_ref, two_ref, three_ref, out_ref, solved):
    own = lax.axis_index("x")
    for step, part in enumerate((own_ref, one_ref, two_ref, three_ref)):
        rows = part[:, which * HALF : (which + 1) * HALF, :]
        solved[pl.ds((own + TURNS - step) % TURNS * PEERS, PEERS)] = rows
    turn(solved, out_ref)


def collect_first(*refs):
    collect(1, *refs)


def collect_second(*refs):
    collect(0, *refs)


def finish(turned_ref, square_ref, new_ref, scale_ref):
    total = jnp.sum(square_ref[:, 0, :], axis=0, keepdims=True)
    scale = jnp.sqrt((total + swap(total)) / ROWS + 1e-06)
    scale_ref[...] = scale[:, :SIDE]
    shape = (SIDE, WIDE)
    row, lane = lax.broadcasted_iota(jnp.int32, shape, 0), lax.broadcasted_iota(jnp.int32, shape, 1)
    down = jnp.sum(jnp.where(row == lane, scale, 0.0), axis=1, keepdims=True)
    new_ref[...] = turned_ref[...] * (1.0 / down)


def struct(*shape):
    return jax.ShapeDtypeStruct(shape, jnp.float32)


def exchange(x, axis):
    return lax.all_to_all(x, axis, 0, 0, tiled=True)


def call(body, *outs):
    return pl.pallas_call(body, out_shape=outs if len(outs) > 1 else outs[0], compiler_params=LIMIT)


def shards(blocks, coords, counts, factor_b, factor_c):
    scalars = pl.BlockSpec(memory_space=pltpu.SMEM)
    local = pl.BlockSpec(memory_space=pltpu.VMEM)
    apart = pl.BlockSpec(memory_space=pltpu.HBM)
    small = (OWNERS, TILE, WIDE)
    full = (OWNERS, HALF, WIDE)
    given = jnp.pad(coords, ((0, SIDE - SLOTS), (SIDE, TILE - 3))).T.astype(jnp.float32)
    row = lax.broadcasted_iota(jnp.int32, given.shape, 0)
    given = jnp.where(row < SIDE, jnp.pad(factor_c, ((0, TILE), (0, 0))), given)
    given = jnp.where(row < SIDE + 3, given, counts.astype(jnp.float32)[:, None])
    opening, place = pl.pallas_call(
        prepare,
        out_shape=(struct(*small), jax.ShapeDtypeStruct((TILE, SIDE), jnp.int32)),
        compiler_params=LIMIT,
    )(given)
    meta = exchange(opening, SLAB)
    gram_b, pairs = pl.pallas_call(
        arrange,
        out_shape=(struct(HALF, WIDE), struct(*full)),
        scratch_shapes=[pltpu.VMEM((2, WIDE, WIDE), jnp.float32)],
        compiler_params=LIMIT,
    )(factor_b.T)
    held = exchange(call(relay, struct(PEERS, HALF + TILE, WIDE))(meta, gram_b), "rows")
    third = exchange(call(answer, struct(*small))(meta, held), SLAB)
    folded, part_a, inverse_a = pl.pallas_call(
        fold,
        in_specs=[scalars, apart, local, local],
        out_specs=[apart, local, local],
        out_shape=(struct(SLOTS, HALF, SIDE, WIDE), struct(*small), struct(WIDE, WIDE)),
        scratch_shapes=[
            pltpu.VMEM((SLOTS, SIDE, SIDE * SIDE), jnp.float32),
            pltpu.VMEM((SLOTS, HALF, SIDE, WIDE), jnp.float32),
            pltpu.VMEM((SLOTS, 2 * WIDE, 2 * WIDE), jnp.bfloat16),
            pltpu.SemaphoreType.DMA((SLOTS,)),
            pltpu.SemaphoreType.DMA((SLOTS,)),
        ],
        compiler_params=LARGE,
    )(place, blocks, third, pairs)
    part_a = exchange(part_a, SLAB)
    answer_a, solved_a = call(solve_first, struct(*small), struct(HALF, WIDE))(part_a, meta, inverse_a)
    first = exchange(answer_a, SLAB)
    first, square_a = lax.optimization_barrier((first, call(share_gram, struct(TILE, WIDE))(first)))
    other_a = lax.ppermute(square_a, "rows", [(n, n ^ 1) for n in range(PEERS)])
    part_b, turned = pl.pallas_call(
        contract,
        in_specs=[apart, local, local],
        out_specs=[local, local],
        out_shape=(struct(*small), jax.ShapeDtypeStruct((WIDE, OWNERS * TILE), jnp.bfloat16)),
        scratch_shapes=[
            pltpu.VMEM((SLOTS, HALF, SIDE, WIDE), jnp.float32),
            pltpu.VMEM((SLOTS, SIDE, WIDE), jnp.float32),
            pltpu.SemaphoreType.DMA((SLOTS,)),
        ],
        compiler_params=LARGE,
    )(folded, first, meta)
    part_b = exchange(call(insert, struct(*small))(part_b, square_a, other_a), SLAB)
    near, square_a = call(sum_second, struct(PEERS, SIDE, WIDE), struct(HALF, WIDE))(part_b, turned, solved_a)
    squares_a = [square_a] + [
        lax.ppermute(square_a, "rows", [(n, (n + 2 * step) % PEERS) for n in range(PEERS)])
        for step in range(1, TURNS)
    ]
    near = exchange(near, "z")
    inverse_b, scale_a = call(invert_second, struct(WIDE, WIDE), struct(1, WIDE))(*squares_a, third)
    near, square_b = call(solve_second, struct(PEERS, SIDE, WIDE), struct(*small))(near, inverse_b, scale_a)
    parts = [near] + [
        lax.ppermute(near, "x", [(n, (n + step) % TURNS) for n in range(TURNS)]) for step in range(1, TURNS)
    ]
    square_b = exchange(square_b, ("x", "rows"))
    scratch = [pltpu.VMEM(full, jnp.float32)]
    new_a, turned_b = (
        pl.pallas_call(body, out_shape=struct(SIDE, GROUP), scratch_shapes=scratch, compiler_params=LIMIT)(*parts)
        for body in (collect_first, collect_second)
    )
    new_b, scale_b = call(finish, struct(SIDE, GROUP), struct(1, SIDE))(turned_b, square_b)
    return (new_a.T, new_b.T, scale_b.reshape(SIDE))


def solution(mesh):
    mesh = Mesh(mesh.devices.reshape(TURNS, PEERS, PEERS), ("x", "z", "rows"))
    split = ("x", "z", "rows")
    in_specs = (P(split, None, None), P(split, None), P(split), P("rows", None), P(split, None))
    out_specs = (P("rows", None), P("rows", None), P())
    return jax.shard_map(shards, mesh=mesh, in_specs=in_specs, out_specs=out_specs, check_vma=False)
```

```python
import jax
import jax.numpy as jnp
from jax import lax
from jax.experimental import pallas as pl
from jax.experimental.pallas import tpu as pltpu
from jax.sharding import Mesh
from jax.sharding import PartitionSpec as P

SIDE = 64
HALF = 32
WIDE = 128
STEP = 8
BEFORE = 14
AFTER = 12
TILE = 8
SLOTS = 6
LEAD = 2
TURNS = 4
PEERS = 8
OWNERS = 32
GROUP = 2048
ROWS = 16384
HIGH = lax.Precision.HIGHEST
SLAB = ("x", "z")
LIMIT = pltpu.CompilerParams(vmem_limit_bytes=24 * 1024 * 1024)
LARGE = pltpu.CompilerParams(vmem_limit_bytes=48 * 1024 * 1024)


def low(shape):
    return lax.broadcasted_iota(jnp.int32, shape, len(shape) - 1) < SIDE


def swap(x):
    return pltpu.roll(x, SIDE, 1)


def unfold_halves(packed):
    mask, other = low(packed.shape), swap(packed)
    return jnp.concatenate([jnp.where(mask, packed, other), jnp.where(mask, other, packed)], axis=0)


def fold_halves(rows):
    return jnp.where(low((HALF, WIDE)), rows[:HALF], rows[HALF:])


def product(left, right, left_dim=1, right_dim=0):
    return lax.dot_general(
        left,
        right,
        (((left_dim,), (right_dim,)), ((), ())),
        precision=HIGH,
        preferred_element_type=jnp.float32,
    )


def gram_packed(packed):
    both = product(packed, packed, 0, 0)
    total = both[:SIDE] + swap(both[SIDE:])
    return fold_halves(jnp.where(low(total.shape), total, swap(total)))


def spot(work, row, lane):
    return jnp.broadcast_to(work[row : row + 1, lane : lane + 1], (TILE, WIDE))


def begin_inverse(gram):
    row = lax.broadcasted_iota(jnp.int32, gram.shape, 0)
    lane = lax.broadcasted_iota(jnp.int32, gram.shape, 1)
    return jnp.where(lane < SIDE, gram, jnp.where(lane - SIDE == row, 1.0, 0.0))


def eliminate(work, first, last):
    row = lax.broadcasted_iota(jnp.int32, work.shape, 0)
    for k in range(first, last):
        line = work[k : k + 1, :] / work[k : k + 1, k : k + 1]
        column = work[:, k : k + 1]
        work = jnp.where(row == k, line, work - column * line)
    return work


def eliminate_all(work):
    row = lax.broadcasted_iota(jnp.int32, work.shape, 0)
    ratio = 1.0 / spot(work, 0, 0)
    for k in range(SIDE):
        line = jnp.broadcast_to(work[k : k + 1, :], (TILE, WIDE)) * ratio
        if k + 1 < SIDE:
            ratio = 1.0 / (spot(work, k + 1, k + 1) - spot(work, k + 1, k) * (spot(work, k, k + 1) * ratio))
        line = jnp.broadcast_to(line[None], (TILE, TILE, WIDE)).reshape(work.shape)
        work = jnp.where(row == k, line, work - work[:, k : k + 1] * line)
    return work


def end_inverse(work):
    zero = jnp.zeros_like(work)
    mask = low(work.shape)
    return jnp.concatenate([jnp.where(mask, swap(work), zero), jnp.where(mask, zero, work)], axis=0)


def inverse(gram):
    return end_inverse(eliminate_all(begin_inverse(gram)))


def held(shape):
    return lax.broadcasted_iota(jnp.int32, shape, 0) % TILE >= LEAD


def pick(meta):
    lane = lax.broadcasted_iota(jnp.int32, meta.shape, 1)
    hit = (meta == (lane % OWNERS).astype(jnp.float32)) & (lane < 2 * OWNERS) & held(meta.shape)
    return jnp.where(hit, 1.0, 0.0)


def choose(chosen, values, chosen_dim=0):
    high = values.astype(jnp.bfloat16)
    rest = values - high.astype(jnp.float32)
    middle = rest.astype(jnp.bfloat16)
    last = (rest - middle.astype(jnp.float32)).astype(jnp.bfloat16)
    parts = lax.dot_general(
        chosen,
        jnp.concatenate([high, middle, last], axis=1),
        (((1 - chosen_dim,), (0,)), ((), ())),
        preferred_element_type=jnp.float32,
    )
    return parts[:, :WIDE] + (parts[:, WIDE : 2 * WIDE] + parts[:, 2 * WIDE :])


def lines(ref):
    return ref[...].reshape(OWNERS * TILE, WIDE)


def prepare(given_ref, out_ref, place_ref):
    third = given_ref[:SIDE, :]
    twice = jnp.concatenate([third, third], axis=1)
    piece, gram = fold_halves(twice), fold_halves(product(third, twice, 0, 0))
    given = given_ref[SIDE:, :].astype(jnp.int32)
    place_ref[...] = given
    row = lax.broadcasted_iota(jnp.int32, given.shape, 0)
    lane = lax.broadcasted_iota(jnp.int32, given.shape, 1)
    first, second, third = (
        jnp.sum(jnp.where(lane == row - LEAD, given[n : n + 1, :], 0), axis=1, keepdims=True) for n in range(3)
    )
    row = lax.broadcasted_iota(jnp.int32, (TILE, WIDE), 0)
    lane = lax.broadcasted_iota(jnp.int32, (TILE, WIDE), 1)
    meta = jnp.where(
        lane < OWNERS,
        first % OWNERS,
        jnp.where(lane < 2 * OWNERS, second % OWNERS, third % PEERS * OWNERS + third // PEERS),
    )
    meta = jnp.where((row >= LEAD) & (row - LEAD < given[3:4, 0:1]), meta, -1)
    out_ref[...] = jnp.broadcast_to(meta.astype(jnp.float32)[None], out_ref.shape)
    out_ref[:, 0, :] = piece
    out_ref[:, 1, :] = gram


def arrange(second_ref, gram_ref, pairs_ref, turned):
    second = second_ref[...]
    gram_ref[...] = fold_halves(product(second, jnp.concatenate([second, second], axis=0), 1, 1))
    mask = low((HALF, WIDE))
    for pair in range(OWNERS // 2):
        tile = second[:, pair * WIDE : (pair + 1) * WIDE]
        turned[pair % 2] = jnp.concatenate([tile, tile], axis=0).T
        for n in range(2):
            even = turned[pair % 2, pl.ds(n * SIDE, HALF, stride=2), :]
            odd = turned[pair % 2, pl.ds(n * SIDE + 1, HALF, stride=2), :]
            pairs_ref[2 * pair + n] = jnp.where(mask, even, odd)


def relay(first_ref, gram_ref, out_ref):
    out_ref[:, :HALF, :] = jnp.broadcast_to(first_ref[:, 0, :][None], (PEERS, HALF, WIDE))
    second = gram_ref[pl.ds(lax.axis_index(SLAB), 1), :]
    third = jnp.sum(first_ref[:, 1, :], axis=0, keepdims=True)
    row = lax.broadcasted_iota(jnp.int32, (TILE, WIDE), 0)
    grams = jnp.where(row == 0, second, jnp.where(row == 1, third, 0.0))
    out_ref[:, HALF:, :] = jnp.broadcast_to(grams[None], (PEERS, TILE, WIDE))


def answer(meta_ref, held_ref, out_ref):
    wanted = lines(meta_ref)[:, 2 * OWNERS : 2 * OWNERS + 1]
    shape = (OWNERS * TILE, PEERS * OWNERS)
    lane = lax.broadcasted_iota(jnp.int32, shape, 1).astype(jnp.float32)
    stock = held_ref[:, :HALF, :].reshape(PEERS * OWNERS, WIDE)
    found = choose(jnp.where((wanted == lane) & held(shape), 1.0, 0.0).astype(jnp.bfloat16), stock)
    grams = jnp.sum(held_ref[:, HALF:, :], axis=0)
    out_ref[...] = found.reshape(OWNERS, TILE, WIDE)
    out_ref[:, 0, :] = jnp.broadcast_to(grams[0:1], (OWNERS, WIDE))
    out_ref[:, 1, :] = jnp.broadcast_to(grams[1:2], (OWNERS, WIDE))


def split(x):
    high = x.astype(jnp.bfloat16)
    return high, (x - high.astype(jnp.float32)).astype(jnp.bfloat16)


def fold(
    place_ref,
    blocks_ref,
    third_ref,
    pairs_ref,
    folded_ref,
    out_ref,
    inverse_ref,
    held,
    made,
    weights,
    held_sem,
    made_sem,
):
    def load(slot):
        return pltpu.make_async_copy(blocks_ref.at[slot], held.at[slot], held_sem.at[slot])

    def store(slot):
        return pltpu.make_async_copy(made.at[slot], folded_ref.at[slot], made_sem.at[slot])

    for slot in range(SLOTS):
        load(slot).start()
    for slot in range(SLOTS):
        packed = third_ref[:, slot + LEAD, :]
        mask, other = low(packed.shape), swap(packed)
        zero = jnp.zeros_like(packed)
        twin = jnp.concatenate(
            [
                jnp.where(mask, packed, zero),
                jnp.where(mask, other, zero),
                jnp.where(mask, zero, other),
                jnp.where(mask, zero, packed),
            ],
            axis=0,
        )
        high, rest = split(twin)
        twin = jnp.concatenate([high, rest], axis=1)
        weights[slot] = jnp.concatenate([twin, twin], axis=0)
    out_ref[:, :LEAD, :] = jnp.zeros((OWNERS, LEAD, WIDE), jnp.float32)
    work = begin_inverse(unfold_halves(third_ref[:, 0, :] * third_ref[:, 1, :]))
    work = eliminate(work, 0, BEFORE)
    groups, inner = SLOTS * HALF // STEP, SIDE - BEFORE - AFTER
    group = 0
    for slot in range(SLOTS):
        pairs = pairs_ref[place_ref[1, slot] % OWNERS]
        load(slot).wait()
        total = jnp.zeros((SIDE, WIDE), jnp.float32)
        for at in range(0, HALF, STEP):
            rows = jnp.concatenate(
                [held[slot, :, (at + n) * WIDE : (at + n + 1) * WIDE] for n in range(STEP)], axis=0
            )
            high, rest = split(rows)
            rows = jnp.concatenate([high, rest], axis=1)
            both = jnp.dot(rows, weights[slot], preferred_element_type=jnp.float32)
            both = both[:, :WIDE] + both[:, WIDE:]
            for n in range(STEP):
                piece = both[n * SIDE : (n + 1) * SIDE]
                made[slot, at + n] = piece
                total += piece * pairs[at + n : at + n + 1, :]
            work = eliminate(work, BEFORE + group * inner // groups, BEFORE + (group + 1) * inner // groups)
            group += 1
        store(slot).start()
        out_ref[:, slot + LEAD, :] = fold_halves(total + swap(total))
    inverse_ref[...] = end_inverse(eliminate(work, SIDE - AFTER, SIDE))
    for slot in range(SLOTS):
        store(slot).wait()


def solve_first(part_ref, meta_ref, inverse_ref, out_ref, solved_ref):
    chosen = pick(lines(meta_ref)).astype(jnp.bfloat16)
    solved = product(choose(chosen, lines(part_ref), 1)[:OWNERS], inverse_ref[...])
    solved_ref[...] = solved
    blank = jnp.zeros((WIDE - OWNERS, WIDE), jnp.float32)
    out_ref[...] = choose(chosen, jnp.concatenate([solved, blank], axis=0)).reshape(OWNERS, TILE, WIDE)
    out_ref[:, 0, :] = gram_packed(solved)


def share_gram(first_ref, out_ref):
    total = jnp.sum(first_ref[:, 0, :], axis=0, keepdims=True)
    out_ref[...] = jnp.broadcast_to(total, out_ref.shape)


def contract(folded_ref, first_ref, meta_ref, out_ref, turned_ref, held, spaced, held_sem):
    def load(slot):
        return pltpu.make_async_copy(folded_ref.at[slot], held.at[slot], held_sem.at[slot])

    for slot in range(SLOTS):
        load(slot).start()
    out_ref[:, :LEAD, :] = jnp.zeros((OWNERS, LEAD, WIDE), jnp.float32)
    turned_ref[...] = pick(lines(meta_ref)).T.astype(jnp.bfloat16)
    for slot in range(SLOTS):
        first = unfold_halves(first_ref[:, slot + LEAD, :])
        load(slot).wait()
        term = jnp.sum(held[slot] * first[None], axis=1)
        spaced[slot, pl.ds(0, HALF, stride=2), :] = term
        spaced[slot, pl.ds(1, HALF, stride=2), :] = swap(term)
        out_ref[:, slot + LEAD, :] = jnp.where(low(term.shape), spaced[slot, :HALF, :], swap(spaced[slot, HALF:, :]))


def insert(part_ref, square_ref, other_ref, out_ref):
    out_ref[...] = part_ref[...]
    out_ref[:, 0, :] = jnp.broadcast_to(square_ref[0:1, :] + other_ref[0:1, :], (OWNERS, WIDE))


def sum_second(part_ref, turned_ref, solved_ref, out_ref, square_ref):
    total = choose(turned_ref[OWNERS : 2 * OWNERS, :], lines(part_ref))
    both = jnp.concatenate([total, solved_ref[...]], axis=0)
    out_ref[...] = jnp.broadcast_to(both[None], out_ref.shape)
    square_ref[...] = part_ref[:, 0, :]


def invert_second(own_ref, one_ref, two_ref, three_ref, third_ref, out_ref, scale_ref):
    square = unfold_halves(own_ref[...] + one_ref[...] + two_ref[...] + three_ref[...])
    shape = square.shape
    row = lax.broadcasted_iota(jnp.int32, shape, 0)
    lane = lax.broadcasted_iota(jnp.int32, shape, 1)
    means = jnp.where(row == lane % SIDE, square, 0.0) / ROWS
    along = jnp.sqrt(jnp.sum(means, axis=0, keepdims=True) + 1e-06)
    down = jnp.sqrt(jnp.sum(jnp.where(lane < SIDE, means, 0.0), axis=1, keepdims=True) + 1e-06)
    scale_ref[...] = 1.0 / along
    out_ref[...] = inverse(square / along / down * unfold_halves(third_ref[:, 1, :]))


def solve_second(near_ref, inverse_ref, scale_ref, out_ref, square_ref):
    near = near_ref[...] * scale_ref[...]
    solved = product(near[:, :HALF].reshape(PEERS * HALF, WIDE), inverse_ref[...])
    out_ref[:, :HALF, :] = solved.reshape(PEERS, HALF, WIDE)
    out_ref[:, HALF:, :] = near[:, HALF:]
    total = jnp.sum(solved * solved, axis=0, keepdims=True)
    square_ref[...] = jnp.broadcast_to(total[None], square_ref.shape)


def turn(solved_ref, out_ref):
    mask = low((HALF, WIDE))
    half = OWNERS // 2
    for pair in range(half // 2):
        parts = []
        for block in (2 * pair, 2 * pair + 1):
            left, right = solved_ref[:, block, :], solved_ref[:, block + half, :]
            parts += [jnp.where(mask, left, swap(right)), jnp.where(mask, swap(left), right)]
        both = jnp.concatenate(parts, axis=0).T
        out_ref[:, pair * WIDE : (pair + 1) * WIDE] = both[:SIDE]
        out_ref[:, GROUP // 2 + pair * WIDE : GROUP // 2 + (pair + 1) * WIDE] = both[SIDE:]


def collect(which, own_ref, one_ref, two_ref, three_ref, out_ref, solved):
    own = lax.axis_index("x")
    for step, part in enumerate((own_ref, one_ref, two_ref, three_ref)):
        rows = part[:, which * HALF : (which + 1) * HALF, :]
        solved[pl.ds((own + TURNS - step) % TURNS * PEERS, PEERS)] = rows
    turn(solved, out_ref)


def collect_first(*refs):
    collect(1, *refs)


def collect_second(*refs):
    collect(0, *refs)


def finish(turned_ref, square_ref, new_ref, scale_ref):
    total = jnp.sum(square_ref[:, 0, :], axis=0, keepdims=True)
    scale = jnp.sqrt((total + swap(total)) / ROWS + 1e-06)
    scale_ref[...] = scale[:, :SIDE]
    shape = (SIDE, WIDE)
    row, lane = lax.broadcasted_iota(jnp.int32, shape, 0), lax.broadcasted_iota(jnp.int32, shape, 1)
    down = jnp.sum(jnp.where(row == lane, scale, 0.0), axis=1, keepdims=True)
    new_ref[...] = turned_ref[...] * (1.0 / down)


def struct(*shape):
    return jax.ShapeDtypeStruct(shape, jnp.float32)


def exchange(x, axis):
    return lax.all_to_all(x, axis, 0, 0, tiled=True)


def call(body, *outs):
    return pl.pallas_call(body, out_shape=outs if len(outs) > 1 else outs[0], compiler_params=LIMIT)


def shards(blocks, coords, counts, factor_b, factor_c):
    scalars = pl.BlockSpec(memory_space=pltpu.SMEM)
    local = pl.BlockSpec(memory_space=pltpu.VMEM)
    apart = pl.BlockSpec(memory_space=pltpu.HBM)
    small = (OWNERS, TILE, WIDE)
    full = (OWNERS, HALF, WIDE)
    given = jnp.pad(coords, ((0, SIDE - SLOTS), (SIDE, TILE - 3))).T.astype(jnp.float32)
    row = lax.broadcasted_iota(jnp.int32, given.shape, 0)
    given = jnp.where(row < SIDE, jnp.pad(factor_c, ((0, TILE), (0, 0))), given)
    given = jnp.where(row < SIDE + 3, given, counts.astype(jnp.float32)[:, None])
    opening, place = pl.pallas_call(
        prepare,
        out_shape=(struct(*small), jax.ShapeDtypeStruct((TILE, SIDE), jnp.int32)),
        compiler_params=LIMIT,
    )(given)
    meta = exchange(opening, SLAB)
    gram_b, pairs = pl.pallas_call(
        arrange,
        out_shape=(struct(HALF, WIDE), struct(*full)),
        scratch_shapes=[pltpu.VMEM((2, WIDE, WIDE), jnp.float32)],
        compiler_params=LIMIT,
    )(factor_b.T)
    held = exchange(call(relay, struct(PEERS, HALF + TILE, WIDE))(meta, gram_b), "rows")
    third = exchange(call(answer, struct(*small))(meta, held), SLAB)
    folded, part_a, inverse_a = pl.pallas_call(
        fold,
        in_specs=[scalars, apart, local, local],
        out_specs=[apart, local, local],
        out_shape=(struct(SLOTS, HALF, SIDE, WIDE), struct(*small), struct(WIDE, WIDE)),
        scratch_shapes=[
            pltpu.VMEM((SLOTS, SIDE, SIDE * SIDE), jnp.float32),
            pltpu.VMEM((SLOTS, HALF, SIDE, WIDE), jnp.float32),
            pltpu.VMEM((SLOTS, 2 * WIDE, 2 * WIDE), jnp.bfloat16),
            pltpu.SemaphoreType.DMA((SLOTS,)),
            pltpu.SemaphoreType.DMA((SLOTS,)),
        ],
        compiler_params=LARGE,
    )(place, blocks, third, pairs)
    part_a = exchange(part_a, SLAB)
    answer_a, solved_a = call(solve_first, struct(*small), struct(HALF, WIDE))(part_a, meta, inverse_a)
    first = exchange(answer_a, SLAB)
    first, square_a = lax.optimization_barrier((first, call(share_gram, struct(TILE, WIDE))(first)))
    other_a = lax.ppermute(square_a, "rows", [(n, n ^ 1) for n in range(PEERS)])
    part_b, turned = pl.pallas_call(
        contract,
        in_specs=[apart, local, local],
        out_specs=[local, local],
        out_shape=(struct(*small), jax.ShapeDtypeStruct((WIDE, OWNERS * TILE), jnp.bfloat16)),
        scratch_shapes=[
            pltpu.VMEM((SLOTS, HALF, SIDE, WIDE), jnp.float32),
            pltpu.VMEM((SLOTS, SIDE, WIDE), jnp.float32),
            pltpu.SemaphoreType.DMA((SLOTS,)),
        ],
        compiler_params=LARGE,
    )(folded, first, meta)
    part_b = exchange(call(insert, struct(*small))(part_b, square_a, other_a), SLAB)
    near, square_a = call(sum_second, struct(PEERS, SIDE, WIDE), struct(HALF, WIDE))(part_b, turned, solved_a)
    squares_a = [square_a] + [
        lax.ppermute(square_a, "rows", [(n, (n + 2 * step) % PEERS) for n in range(PEERS)])
        for step in range(1, TURNS)
    ]
    near = exchange(near, "z")
    inverse_b, scale_a = call(invert_second, struct(WIDE, WIDE), struct(1, WIDE))(*squares_a, third)
    near, square_b = call(solve_second, struct(PEERS, SIDE, WIDE), struct(OWNERS, 1, WIDE))(near, inverse_b, scale_a)
    parts = [near] + [
        lax.ppermute(near, "x", [(n, (n + step) % TURNS) for n in range(TURNS)]) for step in range(1, TURNS)
    ]
    square_b = exchange(square_b, ("x", "rows"))
    scratch = [pltpu.VMEM(full, jnp.float32)]
    new_a, turned_b = (
        pl.pallas_call(body, out_shape=struct(SIDE, GROUP), scratch_shapes=scratch, compiler_params=LIMIT)(*parts)
        for body in (collect_first, collect_second)
    )
    new_b, scale_b = call(finish, struct(SIDE, GROUP), struct(1, SIDE))(turned_b, square_b)
    return (new_a.T, new_b.T, scale_b.reshape(SIDE))


def solution(mesh):
    mesh = Mesh(mesh.devices.reshape(TURNS, PEERS, PEERS), ("x", "z", "rows"))
    split = ("x", "z", "rows")
    in_specs = (P(split, None, None), P(split, None), P(split), P("rows", None), P(split, None))
    out_specs = (P("rows", None), P("rows", None), P())
    return jax.shard_map(shards, mesh=mesh, in_specs=in_specs, out_specs=out_specs, check_vma=False)
```

```python
import jax
import jax.numpy as jnp
from jax import lax
from jax.experimental import pallas as pl
from jax.experimental.pallas import tpu as pltpu
from jax.sharding import Mesh
from jax.sharding import PartitionSpec as P

SIDE = 64
HALF = 32
WIDE = 128
STEP = 8
BEFORE = 14
AFTER = 12
TILE = 8
SLOTS = 6
LEAD = 2
TURNS = 4
PEERS = 8
OWNERS = 32
GROUP = 2048
ROWS = 16384
HIGH = lax.Precision.HIGHEST
SLAB = ("x", "z")
LIMIT = pltpu.CompilerParams(vmem_limit_bytes=24 * 1024 * 1024)
LARGE = pltpu.CompilerParams(vmem_limit_bytes=48 * 1024 * 1024)


def low(shape):
    return lax.broadcasted_iota(jnp.int32, shape, len(shape) - 1) < SIDE


def swap(x):
    return pltpu.roll(x, SIDE, 1)


def unfold_halves(packed):
    mask, other = low(packed.shape), swap(packed)
    return jnp.concatenate([jnp.where(mask, packed, other), jnp.where(mask, other, packed)], axis=0)


def fold_halves(rows):
    return jnp.where(low((HALF, WIDE)), rows[:HALF], rows[HALF:])


def product(left, right, left_dim=1, right_dim=0):
    return lax.dot_general(
        left,
        right,
        (((left_dim,), (right_dim,)), ((), ())),
        precision=HIGH,
        preferred_element_type=jnp.float32,
    )


def gram_packed(packed):
    both = product(packed, packed, 0, 0)
    total = both[:SIDE] + swap(both[SIDE:])
    return fold_halves(jnp.where(low(total.shape), total, swap(total)))


def spot(work, row, lane):
    return jnp.broadcast_to(work[row : row + 1, lane : lane + 1], (TILE, WIDE))


def begin_inverse(gram):
    row = lax.broadcasted_iota(jnp.int32, gram.shape, 0)
    lane = lax.broadcasted_iota(jnp.int32, gram.shape, 1)
    return jnp.where(lane < SIDE, gram, jnp.where(lane - SIDE == row, 1.0, 0.0))


def eliminate(work, first, last):
    row = lax.broadcasted_iota(jnp.int32, work.shape, 0)
    for k in range(first, last):
        line = work[k : k + 1, :] / work[k : k + 1, k : k + 1]
        column = work[:, k : k + 1]
        work = jnp.where(row == k, line, work - column * line)
    return work


def eliminate_all(work):
    row = lax.broadcasted_iota(jnp.int32, (TILE, WIDE), 0)
    tiles = [work[n * TILE : (n + 1) * TILE] for n in range(SIDE // TILE)]
    ratio = 1.0 / spot(tiles[0], 0, 0)
    for k in range(SIDE):
        at, inner = divmod(k, TILE)
        line = jnp.broadcast_to(tiles[at][inner : inner + 1, :], (TILE, WIDE)) * ratio
        if k + 1 < SIDE:
            beside, later = spot(tiles[at], inner, k + 1), divmod(k + 1, TILE)
            ratio = 1.0 / (spot(tiles[later[0]], later[1], k + 1) - beside * (beside * ratio))
        tiles = [tile - tile[:, k : k + 1] * line for tile in tiles]
        tiles[at] = jnp.where(row == inner, line, tiles[at])
    return jnp.concatenate(tiles, axis=0)


def end_inverse(work):
    zero = jnp.zeros_like(work)
    mask = low(work.shape)
    return jnp.concatenate([jnp.where(mask, swap(work), zero), jnp.where(mask, zero, work)], axis=0)


def inverse(gram):
    return end_inverse(eliminate_all(begin_inverse(gram)))


def held(shape):
    return lax.broadcasted_iota(jnp.int32, shape, 0) % TILE >= LEAD


def pick(meta):
    lane = lax.broadcasted_iota(jnp.int32, meta.shape, 1)
    hit = (meta == (lane % OWNERS).astype(jnp.float32)) & (lane < 2 * OWNERS) & held(meta.shape)
    return jnp.where(hit, 1.0, 0.0)


def choose(chosen, values, chosen_dim=0):
    high = values.astype(jnp.bfloat16)
    rest = values - high.astype(jnp.float32)
    middle = rest.astype(jnp.bfloat16)
    last = (rest - middle.astype(jnp.float32)).astype(jnp.bfloat16)
    parts = lax.dot_general(
        chosen,
        jnp.concatenate([high, middle, last], axis=1),
        (((1 - chosen_dim,), (0,)), ((), ())),
        preferred_element_type=jnp.float32,
    )
    return parts[:, :WIDE] + (parts[:, WIDE : 2 * WIDE] + parts[:, 2 * WIDE :])


def lines(ref):
    return ref[...].reshape(OWNERS * TILE, WIDE)


def prepare(given_ref, out_ref, place_ref):
    third = given_ref[:SIDE, :]
    twice = jnp.concatenate([third, third], axis=1)
    piece, gram = fold_halves(twice), fold_halves(product(third, twice, 0, 0))
    given = given_ref[SIDE:, :].astype(jnp.int32)
    place_ref[...] = given
    row = lax.broadcasted_iota(jnp.int32, given.shape, 0)
    lane = lax.broadcasted_iota(jnp.int32, given.shape, 1)
    first, second, third = (
        jnp.sum(jnp.where(lane == row - LEAD, given[n : n + 1, :], 0), axis=1, keepdims=True) for n in range(3)
    )
    row = lax.broadcasted_iota(jnp.int32, (TILE, WIDE), 0)
    lane = lax.broadcasted_iota(jnp.int32, (TILE, WIDE), 1)
    meta = jnp.where(
        lane < OWNERS,
        first % OWNERS,
        jnp.where(lane < 2 * OWNERS, second % OWNERS, third % PEERS * OWNERS + third // PEERS),
    )
    meta = jnp.where((row >= LEAD) & (row - LEAD < given[3:4, 0:1]), meta, -1)
    out_ref[...] = jnp.broadcast_to(meta.astype(jnp.float32)[None], out_ref.shape)
    out_ref[:, 0, :] = piece
    out_ref[:, 1, :] = gram


def arrange(second_ref, gram_ref, pairs_ref, turned):
    second = second_ref[...]
    gram_ref[...] = fold_halves(product(second, jnp.concatenate([second, second], axis=0), 1, 1))
    mask = low((HALF, WIDE))
    for pair in range(OWNERS // 2):
        tile = second[:, pair * WIDE : (pair + 1) * WIDE]
        turned[pair % 2] = jnp.concatenate([tile, tile], axis=0).T
        for n in range(2):
            even = turned[pair % 2, pl.ds(n * SIDE, HALF, stride=2), :]
            odd = turned[pair % 2, pl.ds(n * SIDE + 1, HALF, stride=2), :]
            pairs_ref[2 * pair + n] = jnp.where(mask, even, odd)


def relay(first_ref, gram_ref, out_ref):
    out_ref[:, :HALF, :] = jnp.broadcast_to(first_ref[:, 0, :][None], (PEERS, HALF, WIDE))
    second = gram_ref[pl.ds(lax.axis_index(SLAB), 1), :]
    third = jnp.sum(first_ref[:, 1, :], axis=0, keepdims=True)
    row = lax.broadcasted_iota(jnp.int32, (TILE, WIDE), 0)
    grams = jnp.where(row == 0, second, jnp.where(row == 1, third, 0.0))
    out_ref[:, HALF:, :] = jnp.broadcast_to(grams[None], (PEERS, TILE, WIDE))


def answer(meta_ref, held_ref, out_ref):
    wanted = lines(meta_ref)[:, 2 * OWNERS : 2 * OWNERS + 1]
    shape = (OWNERS * TILE, PEERS * OWNERS)
    lane = lax.broadcasted_iota(jnp.int32, shape, 1).astype(jnp.float32)
    stock = held_ref[:, :HALF, :].reshape(PEERS * OWNERS, WIDE)
    found = choose(jnp.where((wanted == lane) & held(shape), 1.0, 0.0).astype(jnp.bfloat16), stock)
    grams = jnp.sum(held_ref[:, HALF:, :], axis=0)
    out_ref[...] = found.reshape(OWNERS, TILE, WIDE)
    out_ref[:, 0, :] = jnp.broadcast_to(grams[0:1], (OWNERS, WIDE))
    out_ref[:, 1, :] = jnp.broadcast_to(grams[1:2], (OWNERS, WIDE))


def split(x):
    high = x.astype(jnp.bfloat16)
    return high, (x - high.astype(jnp.float32)).astype(jnp.bfloat16)


def fold(
    place_ref,
    blocks_ref,
    third_ref,
    pairs_ref,
    folded_ref,
    out_ref,
    inverse_ref,
    held,
    made,
    weights,
    held_sem,
    made_sem,
):
    def load(slot):
        return pltpu.make_async_copy(blocks_ref.at[slot], held.at[slot], held_sem.at[slot])

    def store(slot):
        return pltpu.make_async_copy(made.at[slot], folded_ref.at[slot], made_sem.at[slot])

    for slot in range(SLOTS):
        load(slot).start()
    for slot in range(SLOTS):
        packed = third_ref[:, slot + LEAD, :]
        mask, other = low(packed.shape), swap(packed)
        zero = jnp.zeros_like(packed)
        twin = jnp.concatenate(
            [
                jnp.where(mask, packed, zero),
                jnp.where(mask, other, zero),
                jnp.where(mask, zero, other),
                jnp.where(mask, zero, packed),
            ],
            axis=0,
        )
        high, rest = split(twin)
        twin = jnp.concatenate([high, rest], axis=1)
        weights[slot] = jnp.concatenate([twin, twin], axis=0)
    out_ref[:, :LEAD, :] = jnp.zeros((OWNERS, LEAD, WIDE), jnp.float32)
    work = begin_inverse(unfold_halves(third_ref[:, 0, :] * third_ref[:, 1, :]))
    work = eliminate(work, 0, BEFORE)
    groups, inner = SLOTS * HALF // STEP, SIDE - BEFORE - AFTER
    group = 0
    for slot in range(SLOTS):
        pairs = pairs_ref[place_ref[1, slot] % OWNERS]
        load(slot).wait()
        total = jnp.zeros((SIDE, WIDE), jnp.float32)
        for at in range(0, HALF, STEP):
            rows = jnp.concatenate(
                [held[slot, :, (at + n) * WIDE : (at + n + 1) * WIDE] for n in range(STEP)], axis=0
            )
            high, rest = split(rows)
            rows = jnp.concatenate([high, rest], axis=1)
            both = jnp.dot(rows, weights[slot], preferred_element_type=jnp.float32)
            both = both[:, :WIDE] + both[:, WIDE:]
            for n in range(STEP):
                piece = both[n * SIDE : (n + 1) * SIDE]
                made[slot, at + n] = piece
                total += piece * pairs[at + n : at + n + 1, :]
            work = eliminate(work, BEFORE + group * inner // groups, BEFORE + (group + 1) * inner // groups)
            group += 1
        store(slot).start()
        out_ref[:, slot + LEAD, :] = fold_halves(total + swap(total))
    inverse_ref[...] = end_inverse(eliminate(work, SIDE - AFTER, SIDE))
    for slot in range(SLOTS):
        store(slot).wait()


def solve_first(part_ref, meta_ref, inverse_ref, out_ref, solved_ref):
    chosen = pick(lines(meta_ref)).astype(jnp.bfloat16)
    solved = product(choose(chosen, lines(part_ref), 1)[:OWNERS], inverse_ref[...])
    solved_ref[...] = solved
    blank = jnp.zeros((WIDE - OWNERS, WIDE), jnp.float32)
    out_ref[...] = choose(chosen, jnp.concatenate([solved, blank], axis=0)).reshape(OWNERS, TILE, WIDE)
    out_ref[:, 0, :] = gram_packed(solved)


def share_gram(first_ref, out_ref):
    total = jnp.sum(first_ref[:, 0, :], axis=0, keepdims=True)
    out_ref[...] = jnp.broadcast_to(total, out_ref.shape)


def contract(folded_ref, first_ref, meta_ref, out_ref, turned_ref, held, spaced, held_sem):
    def load(slot):
        return pltpu.make_async_copy(folded_ref.at[slot], held.at[slot], held_sem.at[slot])

    for slot in range(SLOTS):
        load(slot).start()
    out_ref[:, :LEAD, :] = jnp.zeros((OWNERS, LEAD, WIDE), jnp.float32)
    turned_ref[...] = pick(lines(meta_ref)).T.astype(jnp.bfloat16)
    for slot in range(SLOTS):
        first = unfold_halves(first_ref[:, slot + LEAD, :])
        load(slot).wait()
        term = jnp.sum(held[slot] * first[None], axis=1)
        spaced[slot, pl.ds(0, HALF, stride=2), :] = term
        spaced[slot, pl.ds(1, HALF, stride=2), :] = swap(term)
        out_ref[:, slot + LEAD, :] = jnp.where(low(term.shape), spaced[slot, :HALF, :], swap(spaced[slot, HALF:, :]))


def insert(part_ref, square_ref, other_ref, out_ref):
    out_ref[...] = part_ref[...]
    out_ref[:, 0, :] = jnp.broadcast_to(square_ref[0:1, :] + other_ref[0:1, :], (OWNERS, WIDE))


def sum_second(part_ref, turned_ref, solved_ref, out_ref, square_ref):
    total = choose(turned_ref[OWNERS : 2 * OWNERS, :], lines(part_ref))
    both = jnp.concatenate([total, solved_ref[...]], axis=0)
    out_ref[...] = jnp.broadcast_to(both[None], out_ref.shape)
    square_ref[...] = part_ref[:, 0, :]


def invert_second(own_ref, one_ref, two_ref, three_ref, third_ref, out_ref, scale_ref):
    square = unfold_halves(own_ref[...] + one_ref[...] + two_ref[...] + three_ref[...])
    shape = square.shape
    row = lax.broadcasted_iota(jnp.int32, shape, 0)
    lane = lax.broadcasted_iota(jnp.int32, shape, 1)
    means = jnp.where(row == lane % SIDE, square, 0.0) / ROWS
    along = jnp.sqrt(jnp.sum(means, axis=0, keepdims=True) + 1e-06)
    down = jnp.sqrt(jnp.sum(jnp.where(lane < SIDE, means, 0.0), axis=1, keepdims=True) + 1e-06)
    scale_ref[...] = 1.0 / along
    out_ref[...] = inverse(square / along / down * unfold_halves(third_ref[:, 1, :]))


def solve_second(near_ref, inverse_ref, scale_ref, out_ref, square_ref):
    near = near_ref[...] * scale_ref[...]
    solved = product(near[:, :HALF].reshape(PEERS * HALF, WIDE), inverse_ref[...])
    out_ref[:, :HALF, :] = solved.reshape(PEERS, HALF, WIDE)
    out_ref[:, HALF:, :] = near[:, HALF:]
    total = jnp.sum(solved * solved, axis=0, keepdims=True)
    square_ref[...] = jnp.broadcast_to(total[None], square_ref.shape)


def turn(solved_ref, out_ref):
    mask = low((HALF, WIDE))
    half = OWNERS // 2
    for pair in range(half // 2):
        parts = []
        for block in (2 * pair, 2 * pair + 1):
            left, right = solved_ref[:, block, :], solved_ref[:, block + half, :]
            parts += [jnp.where(mask, left, swap(right)), jnp.where(mask, swap(left), right)]
        both = jnp.concatenate(parts, axis=0).T
        out_ref[:, pair * WIDE : (pair + 1) * WIDE] = both[:SIDE]
        out_ref[:, GROUP // 2 + pair * WIDE : GROUP // 2 + (pair + 1) * WIDE] = both[SIDE:]


def collect(which, own_ref, one_ref, two_ref, three_ref, out_ref, solved):
    own = lax.axis_index("x")
    for step, part in enumerate((own_ref, one_ref, two_ref, three_ref)):
        rows = part[:, which * HALF : (which + 1) * HALF, :]
        solved[pl.ds((own + TURNS - step) % TURNS * PEERS, PEERS)] = rows
    turn(solved, out_ref)


def collect_first(*refs):
    collect(1, *refs)


def collect_second(*refs):
    collect(0, *refs)


def finish(turned_ref, square_ref, new_ref, scale_ref):
    total = jnp.sum(square_ref[:, 0, :], axis=0, keepdims=True)
    scale = jnp.sqrt((total + swap(total)) / ROWS + 1e-06)
    scale_ref[...] = scale[:, :SIDE]
    shape = (SIDE, WIDE)
    row, lane = lax.broadcasted_iota(jnp.int32, shape, 0), lax.broadcasted_iota(jnp.int32, shape, 1)
    down = jnp.sum(jnp.where(row == lane, scale, 0.0), axis=1, keepdims=True)
    new_ref[...] = turned_ref[...] * (1.0 / down)


def struct(*shape):
    return jax.ShapeDtypeStruct(shape, jnp.float32)


def exchange(x, axis):
    return lax.all_to_all(x, axis, 0, 0, tiled=True)


def call(body, *outs):
    return pl.pallas_call(body, out_shape=outs if len(outs) > 1 else outs[0], compiler_params=LIMIT)


def shards(blocks, coords, counts, factor_b, factor_c):
    scalars = pl.BlockSpec(memory_space=pltpu.SMEM)
    local = pl.BlockSpec(memory_space=pltpu.VMEM)
    apart = pl.BlockSpec(memory_space=pltpu.HBM)
    small = (OWNERS, TILE, WIDE)
    full = (OWNERS, HALF, WIDE)
    given = jnp.pad(coords, ((0, SIDE - SLOTS), (SIDE, TILE - 3))).T.astype(jnp.float32)
    row = lax.broadcasted_iota(jnp.int32, given.shape, 0)
    given = jnp.where(row < SIDE, jnp.pad(factor_c, ((0, TILE), (0, 0))), given)
    given = jnp.where(row < SIDE + 3, given, counts.astype(jnp.float32)[:, None])
    opening, place = pl.pallas_call(
        prepare,
        out_shape=(struct(*small), jax.ShapeDtypeStruct((TILE, SIDE), jnp.int32)),
        compiler_params=LIMIT,
    )(given)
    meta = exchange(opening, SLAB)
    gram_b, pairs = pl.pallas_call(
        arrange,
        out_shape=(struct(HALF, WIDE), struct(*full)),
        scratch_shapes=[pltpu.VMEM((2, WIDE, WIDE), jnp.float32)],
        compiler_params=LIMIT,
    )(factor_b.T)
    held = exchange(call(relay, struct(PEERS, HALF + TILE, WIDE))(meta, gram_b), "rows")
    third = exchange(call(answer, struct(*small))(meta, held), SLAB)
    folded, part_a, inverse_a = pl.pallas_call(
        fold,
        in_specs=[scalars, apart, local, local],
        out_specs=[apart, local, local],
        out_shape=(struct(SLOTS, HALF, SIDE, WIDE), struct(*small), struct(WIDE, WIDE)),
        scratch_shapes=[
            pltpu.VMEM((SLOTS, SIDE, SIDE * SIDE), jnp.float32),
            pltpu.VMEM((SLOTS, HALF, SIDE, WIDE), jnp.float32),
            pltpu.VMEM((SLOTS, 2 * WIDE, 2 * WIDE), jnp.bfloat16),
            pltpu.SemaphoreType.DMA((SLOTS,)),
            pltpu.SemaphoreType.DMA((SLOTS,)),
        ],
        compiler_params=LARGE,
    )(place, blocks, third, pairs)
    part_a = exchange(part_a, SLAB)
    answer_a, solved_a = call(solve_first, struct(*small), struct(HALF, WIDE))(part_a, meta, inverse_a)
    first = exchange(answer_a, SLAB)
    first, square_a = lax.optimization_barrier((first, call(share_gram, struct(1, WIDE))(first)))
    other_a = lax.ppermute(square_a, "rows", [(n, n ^ 1) for n in range(PEERS)])
    part_b, turned = pl.pallas_call(
        contract,
        in_specs=[apart, local, local],
        out_specs=[local, local],
        out_shape=(struct(*small), jax.ShapeDtypeStruct((WIDE, OWNERS * TILE), jnp.bfloat16)),
        scratch_shapes=[
            pltpu.VMEM((SLOTS, HALF, SIDE, WIDE), jnp.float32),
            pltpu.VMEM((SLOTS, SIDE, WIDE), jnp.float32),
            pltpu.SemaphoreType.DMA((SLOTS,)),
        ],
        compiler_params=LARGE,
    )(folded, first, meta)
    part_b = exchange(call(insert, struct(*small))(part_b, square_a, other_a), SLAB)
    near, square_a = call(sum_second, struct(PEERS, SIDE, WIDE), struct(HALF, WIDE))(part_b, turned, solved_a)
    squares_a = [square_a] + [
        lax.ppermute(square_a, "rows", [(n, (n + 2 * step) % PEERS) for n in range(PEERS)])
        for step in range(1, TURNS)
    ]
    near = exchange(near, "z")
    inverse_b, scale_a = call(invert_second, struct(WIDE, WIDE), struct(1, WIDE))(*squares_a, third)
    near, square_b = call(solve_second, struct(PEERS, SIDE, WIDE), struct(OWNERS, 1, WIDE))(near, inverse_b, scale_a)
    parts = [near] + [
        lax.ppermute(near, "x", [(n, (n + step) % TURNS) for n in range(TURNS)]) for step in range(1, TURNS)
    ]
    square_b = exchange(square_b, ("x", "rows"))
    scratch = [pltpu.VMEM(full, jnp.float32)]
    new_a, turned_b = (
        pl.pallas_call(body, out_shape=struct(SIDE, GROUP), scratch_shapes=scratch, compiler_params=LIMIT)(*parts)
        for body in (collect_first, collect_second)
    )
    new_b, scale_b = call(finish, struct(SIDE, GROUP), struct(1, SIDE))(turned_b, square_b)
    return (new_a.T, new_b.T, scale_b.reshape(SIDE))


def solution(mesh):
    mesh = Mesh(mesh.devices.reshape(TURNS, PEERS, PEERS), ("x", "z", "rows"))
    split = ("x", "z", "rows")
    in_specs = (P(split, None, None), P(split, None), P(split), P("rows", None), P(split, None))
    out_specs = (P("rows", None), P("rows", None), P())
    return jax.shard_map(shards, mesh=mesh, in_specs=in_specs, out_specs=out_specs, check_vma=False)
```
